512 devices in a mesh: chan: 8 (over x, z_hi), seq: 64 (over y, z_lo, core).
Axes of the slice: x: 4, y: 8, z: 8 (z_hi: 2, z_lo: 4; z = z_hi * 4 + z_lo), core: 2. Of those that a mesh axis runs over, the one named last changes fastest.
Arguments:
- signal: bfloat16 [524288, 1024], P('seq', 'chan'), may hold values from -6 to 6
- cotangent: bfloat16 [524288, 1024], P('seq', 'chan'), may hold values from -6 to 6
- depth_factor: bfloat16 [64, 64], replicated, may hold values from -0.75 to 0.75
- column_factor: bfloat16 [64, 64], replicated, may hold values from -0.75 to 0.75
- row_factor: bfloat16 [128, 128], replicated, may hold values from -0.5 to 0.5
- depth_mask: int32 [4, 4], replicated, may hold values 0 or 1
- column_mask: int32 [4, 4], replicated, may hold values 0 or 1
- row_mask: int32 [8, 8], replicated, may hold values 0 or 1
Outputs:
- grad_depth: float32 [64, 64], replicated
- grad_column: float32 [64, 64], replicated
- grad_row: float32 [128, 128], replicated
The draws below stay inside these ranges and needn't reach their ends.
Inputs may be any that keep to these rules, and one draw needn't show every extreme that they name: `depth_mask`: entry 1 keeps a 16 x 16 tile of the factor. `column_mask`: entry 1 keeps a 16 x 16 tile of the factor. `row_mask`: entry 1 keeps a 16 x 16 tile of the factor.
All inputs are finite; a program needn't handle non-finite values.
Results may differ from the reference program's by a relative error of at most 0.0055.
Values may be sent and summed in bfloat16 or wider, within the bound.
A program may use at most 64 MiB of HBM per device.

```python
import math
import jax
import jax.numpy as jnp
from jax import lax

OUTER = 128
MIDDLE = 64
INNER = 64
CHANNELS = 1024
TILE = 16
SEQLEN = 524288


def set_ends(values, rng, least, largest):
    longest = values.shape.index(max(values.shape))
    spots = []
    for shift in (0, 1):
        where = [jax.random.randint(jax.random.fold_in(rng, axis), (), 0, length) for axis, length in enumerate(values.shape)]
        where[longest] = (where[longest] + shift) % values.shape[longest]
        spots.append(tuple(where))
    return values.at[spots[0]].set(least).at[spots[1]].set(largest)


def levels(stream_key, shape, pieces, low, top_value):
    factor_of, own = 1.0, jax.random.fold_in(stream_key, 6)
    for dim, parts in pieces:
        draws = jnp.exp(jax.random.uniform(jax.random.fold_in(own, dim), (parts,), jnp.float32, low / len(pieces), top_value / len(pieces)))
        factor_of = factor_of * jnp.repeat(draws, shape[dim] // parts).reshape([-1 if axis == dim else 1 for axis in range(len(shape))])
    return factor_of


def centred(own_key, shape, spread, bound, shards=(), dtype=jnp.bfloat16):
    gain = levels(own_key, shape, shards, -0.22, 0.18) if shards else 1.0
    array = jax.random.normal(own_key, shape, jnp.float32) * spread * gain
    return jnp.minimum(jnp.maximum(array, -bound), bound).astype(dtype)


def setup_inputs(seed: int = 0) -> dict:
    keys = jax.random.split(jax.random.key(seed), 9)
    return {
        "signal": centred(keys[0], (SEQLEN, CHANNELS), 1.0, 6.0, ((0, 64), (1, 8))),
        "cotangent": centred(keys[1], (SEQLEN, CHANNELS), 1.0, 6.0, ((0, 64), (1, 8))),
        "depth_factor": centred(keys[2], (INNER, INNER), INNER ** -0.5, 0.75),
        "column_factor": centred(keys[3], (MIDDLE, MIDDLE), MIDDLE ** -0.5, 0.75),
        "row_factor": centred(keys[4], (OUTER, OUTER), OUTER ** -0.5, 0.5),
        "depth_mask": set_ends((jax.random.randint(keys[5], (INNER // TILE, INNER // TILE), 0, 4) < 3).astype(jnp.int32), jax.random.fold_in(keys[5], 1), 0, 1),
        "column_mask": set_ends((jax.random.randint(keys[6], (MIDDLE // TILE, MIDDLE // TILE), 0, 4) < 3).astype(jnp.int32), jax.random.fold_in(keys[6], 1), 0, 1),
        "row_mask": set_ends((jax.random.randint(keys[7], (OUTER // TILE, OUTER // TILE), 0, 4) < 3).astype(jnp.int32), jax.random.fold_in(keys[7], 1), 0, 1),
    }


def spread_mask(mask, weight):
    factor = weight.shape[0] // mask.shape[0]
    return jnp.repeat(jnp.repeat(mask, factor, axis=0), factor, axis=1)

def masked(weight, mask):
    return jnp.where(spread_mask(mask, weight) == 1, weight, jnp.zeros_like(weight))

def finish(grad, mask, length):
    count = SEQLEN * CHANNELS // length
    scaled = grad * (1.0 / math.sqrt(count))
    return jnp.where(spread_mask(mask, grad) == 1, scaled, jnp.zeros_like(scaled))

def reference(signal, cotangent, depth_factor, column_factor, row_factor, depth_mask, column_mask, row_mask):
    w_depth = masked(depth_factor, depth_mask).astype(jnp.float32)
    w_column = masked(column_factor, column_mask).astype(jnp.float32)
    w_row = masked(row_factor, row_mask).astype(jnp.float32)
    width = min(CHANNELS, 128)
    blocks = CHANNELS // width
    fields = jnp.moveaxis(signal.reshape(OUTER, MIDDLE, INNER, blocks, width), 3, 0)
    uppers = jnp.moveaxis(cotangent.reshape(OUTER, MIDDLE, INNER, blocks, width), 3, 0)

    def step(carry, pair):
        acc_row, acc_column, acc_depth = carry
        field = pair[0].astype(jnp.float32)
        upstream = pair[1].astype(jnp.float32)
        first = jnp.einsum('pq,ijqc->ijpc', w_depth, field).astype(jnp.bfloat16).astype(jnp.float32)
        second = jnp.einsum('pq,iqkc->ipkc', w_column, first).astype(jnp.bfloat16).astype(jnp.float32)
        gated = (upstream * field).astype(jnp.bfloat16).astype(jnp.float32)
        acc_row = acc_row + jnp.einsum('iabc,jabc->ij', gated, second)
        back_second = jnp.einsum('pi,pabc->iabc', w_row, gated).astype(jnp.bfloat16).astype(jnp.float32)
        acc_column = acc_column + jnp.einsum('iakc,ibkc->ab', back_second, first)
        back_first = jnp.einsum('pq,ipkc->iqkc', w_column, back_second).astype(jnp.bfloat16).astype(jnp.float32)
        acc_depth = acc_depth + jnp.einsum('ijpc,ijqc->pq', back_first, field)
        return ((acc_row, acc_column, acc_depth), None)
    start = (jnp.zeros((OUTER, OUTER), jnp.float32), jnp.zeros((MIDDLE, MIDDLE), jnp.float32), jnp.zeros((INNER, INNER), jnp.float32))
    (acc_row, acc_column, acc_depth), _ = lax.scan(step, start, (fields, uppers))
    grad_depth = finish(acc_depth, depth_mask, INNER)
    grad_column = finish(acc_column, column_mask, MIDDLE)
    grad_row = finish(acc_row, row_mask, OUTER)
    return (grad_depth, grad_column, grad_row)
```

```python
import functools
import math

import jax
import jax.numpy as jnp
from jax import lax
from jax.experimental import pallas as pl
from jax.experimental.pallas import tpu as pltpu
from jax.sharding import PartitionSpec as P

CHANNELS = 1024
SEQLEN = 524288
MIDDLE = 64
INNER = 64
LANES = 128
X, ZH, Y, ZL, CORES = 4, 2, 8, 4, 2
CHUNK = 16
Y_ORDER = (1, 7, 2, 6, 3, 5, 4, 0)
F32, BF16 = jnp.float32, jnp.bfloat16
MESH = pl.DeviceIdType.MESH


def dot(a, b, contract):
    return lax.dot_general(a, b, ((contract[:1], contract[1:]), ((), ())), preferred_element_type=F32)


def iota(shape, axis):
    return lax.broadcasted_iota(jnp.int32, shape, axis)


def onehot(shape, left, right):
    return jnp.where(left(iota(shape, 0)) == right(iota(shape, 1)), 1.0, 0.0)


def same(value):
    return value


def spread_mask(mask_ref, size):
    tiles = mask_ref.shape[0]
    side = size // tiles
    mask = jnp.where(mask_ref[...] == 1, 1.0, 0.0)
    rows = onehot((size, tiles), lambda r: r // side, same)
    columns = onehot((tiles, size), same, lambda c: c // side)
    return dot(dot(rows, mask, (1, 0)), columns, (1, 0))


def twice(weight):
    size = weight.shape[0]
    rows = onehot((2 * size, size), lambda r: r % size, same).astype(BF16)
    columns = onehot((size, 2 * size), same, lambda c: c % size).astype(BF16)
    full = dot(dot(rows, weight, (1, 0)).astype(BF16), columns, (1, 0))
    return (full * onehot(full.shape, lambda r: r // size, lambda c: c // size)).astype(BF16)


def kernel(
    seqs, outer, chunk,
    signal_hbm, cotangent_hbm, depth_ref, column_ref, row_ref, depth_mask, column_mask, row_mask,
    out_depth, out_column, out_row,
    signal, cotangent, flipped, send_x, send_g, got_x, got_g, first, mixed, second, wide, back,
    w_row_t, w_depth2, w_column2, parts, land_1, land_2, land_3, land_4, sum_1, sum_2, sum_3,
    load_sem, self_sem, send_sem, recv_sem, part_send, part_recv,
):
    jk = MIDDLE * INNER
    chunks = MIDDLE // chunk
    pair = 2 * chunk
    width = 2 * seqs
    ring = ZL * CORES
    chan, me = lax.axis_index("chan"), lax.axis_index("seq")
    x, z_hi = chan // ZH, chan % ZH
    y, inner = me // ring, me % ring
    z_lo, core = inner // CORES, inner % CORES
    z = z_hi * ZL + z_lo
    local_rows = (outer + MIDDLE) // Y

    load_x = pltpu.make_async_copy(signal_hbm, signal, load_sem.at[0])
    load_c = pltpu.make_async_copy(cotangent_hbm, cotangent, load_sem.at[1])
    load_x.start()
    load_c.start()

    def y_peer(step):
        return chan, lax.rem(y + step, Y) * ring + inner

    def z_peer(step):
        there = lax.rem(z + step, ZH * ZL)
        return x * ZH + there // ZL, y * ring + lax.rem(there, ZL) * CORES + core

    def x_peer(step):
        there = lax.rem(x * CORES + core + step, X * CORES)
        return there // CORES * ZH + z_hi, y * ring + z_lo * CORES + lax.rem(there, CORES)

    barrier = pltpu.get_barrier_semaphore()

    @pl.loop(1, seqs)
    def _(step):
        pl.semaphore_signal(barrier, inc=1, device_id=(chan, lax.rem(me + step, seqs)), device_id_type=MESH)

    greeted = seqs - 1
    for away in range(ZL):
        if ZH == 2:
            pl.semaphore_signal(
                barrier, inc=1,
                device_id=(x * ZH + 1 - z_hi, y * ring + away * CORES + core), device_id_type=MESH,
            )
            greeted += 1
    for step in range(1, X):
        for other in range(CORES):
            there = lax.rem(x + step, X) * ZH + z_hi
            pl.semaphore_signal(
                barrier, inc=1, device_id=(there, y * ring + z_lo * CORES + other), device_id_type=MESH
            )
            greeted += 1

    pick = onehot((seqs, width), same, lambda c: c // 2).astype(BF16)
    even = jnp.where(iota((1, width), 1) % 2 == 0, 1.0, 0.0).astype(BF16)
    odd = jnp.where(iota((1, width), 1) % 2 == 1, 1.0, 0.0).astype(BF16)

    def flip(read):
        def body(block, carry):
            value = read(pl.ds(pl.multiple_of(block * INNER, INNER), INNER))
            both = jnp.concatenate([value * even, value * odd], axis=0)
            flipped[pl.ds(pl.multiple_of(block * seqs, seqs), seqs), :] = dot(pick, both, (1, 1))
            return carry

        lax.fori_loop(0, 2 * MIDDLE, body, 0, unroll=8)

    def send(source, target, slot, run):
        def body(turn, carry):
            for place, away in enumerate(Y_ORDER):
                if away >= Y:
                    continue
                step = lax.rem(turn + place + 1, ring)
                to = lax.rem(y + away, Y) * ring + lax.rem(inner + step, ring)

                def go():
                    pltpu.make_async_remote_copy(
                        src_ref=source(to), dst_ref=target(me),
                        send_sem=send_sem.at[slot], recv_sem=recv_sem.at[slot],
                        device_id=(chan, to), device_id_type=MESH,
                    ).start()

                if away == 0:
                    pl.when(step != 0)(go)
                else:
                    go()
            return carry

        lax.fori_loop(0, ring, body, 0)
        return run

    load_x.wait()
    flip(lambda rows: signal[rows, :])

    def pack_x(d, carry):
        send_x[d] = flipped[pl.ds(d, 2 * MIDDLE, stride=seqs), :].astype(BF16)
        return carry

    lax.fori_loop(0, seqs, pack_x, 0, unroll=4)
    pl.semaphore_wait(barrier, greeted)
    send(lambda to: send_x.at[to], lambda at: got_x.at[at], 0, None)
    own_x = pltpu.make_async_copy(send_x.at[me], got_x.at[me], self_sem.at[0])
    own_x.start()

    load_c.wait()
    flip(lambda rows: (cotangent[rows, :].astype(F32) * signal[rows, :].astype(F32)).astype(BF16))
    owns = []
    for part in range(chunks):
        def pack_g(d, carry):
            for i in range(2):
                start = (i * MIDDLE + part * chunk) * seqs + d
                send_g[part, d, i * chunk : (i + 1) * chunk, :] = flipped[
                    pl.ds(start, chunk, stride=seqs), :
                ].astype(BF16)
            return carry

        lax.fori_loop(0, seqs, pack_g, 0, unroll=4)
        send(lambda to: send_g.at[part, to], lambda at: got_g.at[part, at], 1 + part, None)
        own = pltpu.make_async_copy(send_g.at[part, me], got_g.at[part, me], self_sem.at[1 + part])
        own.start()
        owns.append(own)

    keep_row = spread_mask(row_mask, outer)
    keep_column = spread_mask(column_mask, MIDDLE)
    keep_depth = spread_mask(depth_mask, INNER)
    w_row = (row_ref[...].astype(F32) * keep_row).astype(BF16)
    w_row_t[...] = dot(onehot((outer, outer), same, same).astype(BF16), w_row, (1, 1)).astype(BF16)
    w_depth2[...] = twice((depth_ref[...].astype(F32) * keep_depth).astype(BF16))
    w_column2[...] = twice((column_ref[...].astype(F32) * keep_column).astype(BF16))

    def arrived(ref, sem):
        others = ref.at[pl.ds(0, seqs - 1)]
        pltpu.make_async_copy(others, others, sem).wait()

    own_x.wait()
    arrived(got_x, recv_sem.at[0])

    def signal_side(s, carry):
        field = got_x[s]
        one = dot(field, w_depth2[...], (1, 1)).astype(BF16)
        first[s] = one
        two = dot(w_column2[...], jnp.concatenate([field, one], axis=1), (1, 0))
        for part in range(chunks):
            for i in range(2):
                mixed[part, s, i * chunk : (i + 1) * chunk, :] = two[
                    i * MIDDLE + part * chunk : i * MIDDLE + (part + 1) * chunk, :LANES
                ].astype(BF16)
        wide[pl.ds(pl.multiple_of(s * 2 * MIDDLE, 2 * MIDDLE), 2 * MIDDLE), :] = two[:, LANES:]
        return carry

    lax.fori_loop(0, seqs, signal_side, 0, unroll=4)

    def by_column(j, carry):
        second[j] = wide[pl.ds(j, outer, stride=MIDDLE), :].astype(BF16)
        return carry

    lax.fori_loop(0, MIDDLE, by_column, 0, unroll=4)

    grad_row = jnp.zeros((outer, outer), F32)
    grad_depth = jnp.zeros((LANES, LANES), F32)
    group = min(4, seqs)
    for part in range(chunks):
        owns[part].wait()
        arrived(got_g.at[part], recv_sem.at[1 + part])

        def widen(s, carry):
            wide[pl.ds(pl.multiple_of(s * pair, pair), pair), :] = got_g[part, s].astype(F32)
            return carry

        lax.fori_loop(0, seqs, widen, 0, unroll=8)

        def row_side(j, total):
            gated = wide[pl.ds(j, outer, stride=chunk), :].astype(BF16)
            back[pl.ds(j, outer, stride=chunk), :] = dot(w_row_t[...], gated, (1, 0))
            return total + dot(gated, second[part * chunk + j], (1, 1))

        grad_row = lax.fori_loop(0, chunk, row_side, grad_row, unroll=4)

        def back_side(block, carry):
            column, depth = carry
            rows = group * pair
            value = back[pl.ds(pl.multiple_of(block * rows, rows), rows), :].astype(BF16)
            fields = mixed[part, pl.ds(block * group, group)].reshape(rows, LANES)
            depth = depth + dot(value, fields, (0, 0))
            ours, theirs = [], []
            for s in range(group):
                at = s * pair
                ours.append(jnp.concatenate([value[at : at + chunk], value[at + chunk : at + pair]], axis=1))
                one = first[block * group + s]
                theirs.append(jnp.concatenate([one[:MIDDLE], one[MIDDLE:]], axis=1))
            column = column + dot(jnp.concatenate(ours, axis=0), jnp.concatenate(theirs, axis=0), (1, 1))
            return column, depth

        column, grad_depth = lax.fori_loop(
            0, seqs // group, back_side,
            (jnp.zeros((group * chunk, group * MIDDLE), F32), grad_depth), unroll=2,
        )
        piece = jnp.zeros((chunk, MIDDLE), F32)
        for s in range(group):
            piece = piece + column[s * chunk : (s + 1) * chunk, s * MIDDLE : (s + 1) * MIDDLE]
        parts[outer + part * chunk : outer + (part + 1) * chunk, :MIDDLE] = piece
    parts[:outer, :outer] = grad_row
    parts[outer:, MIDDLE:] = grad_depth[:INNER, :INNER] + grad_depth[INNER:, INNER:]

    def exchange(phase, count, peer, source, target):
        copies = []
        for step in range(1, count):
            to = peer(step)
            copy = pltpu.make_async_remote_copy(
                src_ref=source(to), dst_ref=target,
                send_sem=part_send.at[phase], recv_sem=part_recv.at[phase],
                device_id=to, device_id_type=MESH,
            )
            copy.start()
            copies.append(copy)

    def landed(phase, land, count):
        others = land.at[pl.ds(0, count - 1)]
        pltpu.make_async_copy(others, others, part_recv.at[phase]).wait()

    def added(land):
        total = land[0]
        for slot in range(1, land.shape[0]):
            total = total + land[slot]
        return total

    def rows_of(place):
        return pl.ds(pl.multiple_of(place * local_rows, 8), local_rows)

    land_1[y] = parts[rows_of(y), :]
    exchange(0, Y, y_peer, lambda to: parts.at[rows_of(to[1] // ring)], land_1.at[y])
    landed(0, land_1, Y)
    sum_1[...] = added(land_1)
    land_2[z] = sum_1[...]
    exchange(1, ZH * ZL, z_peer, lambda to: sum_1, land_2.at[z])
    landed(1, land_2, ZH * ZL)
    sum_2[...] = added(land_2)
    place = x * CORES + core
    land_3[place] = sum_2[...]
    exchange(2, X * CORES, x_peer, lambda to: sum_2, land_3.at[place])
    landed(2, land_3, X * CORES)
    sum_3[...] = added(land_3)
    land_4[y] = sum_3[...]
    exchange(3, Y, y_peer, lambda to: sum_3, land_4.at[y])
    landed(3, land_4, Y)

    whole = land_4[...].reshape(outer + MIDDLE, LANES)
    inner_count = 1.0 / math.sqrt(SEQLEN * CHANNELS // MIDDLE)
    outer_count = 1.0 / math.sqrt(SEQLEN * CHANNELS // outer)
    out_row[...] = jnp.where(keep_row > 0.5, whole[:outer, :outer] * outer_count, 0.0)
    out_column[...] = jnp.where(keep_column > 0.5, whole[outer:, :MIDDLE] * inner_count, 0.0)
    out_depth[...] = jnp.where(keep_depth > 0.5, whole[outer:, MIDDLE:] * inner_count, 0.0)

    def sent(ref, sem):
        others = ref.at[pl.ds(0, seqs - 1)]
        pltpu.make_async_copy(others, others, sem).wait()

    sent(send_x, send_sem.at[0])
    for part in range(chunks):
        sent(send_g.at[part], send_sem.at[1 + part])
    for phase, (land, count) in enumerate(
        ((land_1, Y), (land_2, ZH * ZL), (land_3, X * CORES), (land_4, Y))
    ):
        others = land.at[pl.ds(0, count - 1)]
        pltpu.make_async_copy(others, others, part_send.at[phase]).wait()


def per_device(
    signal, cotangent, depth_factor, column_factor, row_factor, depth_mask, column_mask, row_mask
):
    seqs = Y * ZL * CORES
    outer = row_factor.shape[0]
    chunk = CHUNK
    chunks = MIDDLE // chunk
    pair = 2 * chunk
    rows, width = signal.shape
    local_rows = (outer + MIDDLE) // Y
    vmem = pl.BlockSpec(memory_space=pltpu.VMEM)
    hbm = pl.BlockSpec(memory_space=pl.ANY)
    return pl.pallas_call(
        functools.partial(kernel, seqs, outer, chunk),
        out_shape=(
            jax.ShapeDtypeStruct((INNER, INNER), F32),
            jax.ShapeDtypeStruct((MIDDLE, MIDDLE), F32),
            jax.ShapeDtypeStruct((outer, outer), F32),
        ),
        in_specs=[hbm, hbm] + [vmem] * 6,
        out_specs=(vmem, vmem, vmem),
        scratch_shapes=[
            pltpu.VMEM((rows, width), BF16),
            pltpu.VMEM((rows, width), BF16),
            pltpu.VMEM((2 * MIDDLE * seqs, LANES), F32),
            pltpu.VMEM((seqs, 2 * MIDDLE, LANES), BF16),
            pltpu.VMEM((chunks, seqs, pair, LANES), BF16),
            pltpu.VMEM((seqs, 2 * MIDDLE, LANES), BF16),
            pltpu.VMEM((chunks, seqs, pair, LANES), BF16),
            pltpu.VMEM((seqs, 2 * MIDDLE, LANES), BF16),
            pltpu.VMEM((chunks, seqs, pair, LANES), BF16),
            pltpu.VMEM((MIDDLE, outer, LANES), BF16),
            pltpu.VMEM((outer * MIDDLE, LANES), F32),
            pltpu.VMEM((outer * chunk, LANES), F32),
            pltpu.VMEM((outer, outer), BF16),
            pltpu.VMEM((LANES, LANES), BF16),
            pltpu.VMEM((LANES, LANES), BF16),
            pltpu.VMEM((outer + MIDDLE, LANES), F32),
            pltpu.VMEM((Y, local_rows, LANES), F32),
            pltpu.VMEM((ZH * ZL, local_rows, LANES), F32),
            pltpu.VMEM((X * CORES, local_rows, LANES), F32),
            pltpu.VMEM((Y, local_rows, LANES), F32),
            pltpu.VMEM((local_rows, LANES), F32),
            pltpu.VMEM((local_rows, LANES), F32),
            pltpu.VMEM((local_rows, LANES), F32),
            pltpu.SemaphoreType.DMA((2,)),
            pltpu.SemaphoreType.DMA((1 + chunks,)),
            pltpu.SemaphoreType.DMA((1 + chunks,)),
            pltpu.SemaphoreType.DMA((1 + chunks,)),
            pltpu.SemaphoreType.DMA((4,)),
            pltpu.SemaphoreType.DMA((4,)),
        ],
        compiler_params=pltpu.CompilerParams(
            collective_id=0, has_side_effects=True, vmem_limit_bytes=48 * 2**20
        ),
        cost_estimate=pl.CostEstimate(flops=1_300_000_000, bytes_accessed=4 * 2**20, transcendentals=0),
    )(signal, cotangent, depth_factor, column_factor, row_factor, depth_mask, column_mask, row_mask)


def solution(mesh):
    in_specs = (P("seq", "chan"), P("seq", "chan"), P(), P(), P(), P(), P(), P())
    out_specs = (P(), P(), P())
    return jax.shard_map(
        per_device, mesh=mesh, in_specs=in_specs, out_specs=out_specs, check_vma=False
    )
```

```python
import functools
import math

import jax
import jax.numpy as jnp
from jax import lax
from jax.experimental import pallas as pl
from jax.experimental.pallas import tpu as pltpu
from jax.sharding import PartitionSpec as P

CHANNELS = 1024
SEQLEN = 524288
MIDDLE = 64
INNER = 64
LANES = 128
X, ZH, Y, ZL, CORES = 4, 2, 8, 4, 2
PARTS = (16, 16, 16, 8, 8)
Y_ORDER = (1, 7, 2, 6, 3, 5, 4, 0)
FAR_FIRST = (4, 3, 5, 2, 6, 1, 7)
F32, BF16 = jnp.float32, jnp.bfloat16
MESH = pl.DeviceIdType.MESH


def dot(a, b, contract):
    return lax.dot_general(a, b, ((contract[:1], contract[1:]), ((), ())), preferred_element_type=F32)


def iota(shape, axis):
    return lax.broadcasted_iota(jnp.int32, shape, axis)


def onehot(shape, left, right):
    return jnp.where(left(iota(shape, 0)) == right(iota(shape, 1)), 1.0, 0.0)


def same(value):
    return value


def spread_mask(mask, size):
    tiles = mask.shape[0]
    side = size // tiles
    ones = jnp.where(mask == 1, 1.0, 0.0)
    rows = onehot((size, tiles), lambda r: r // side, same)
    columns = onehot((tiles, size), same, lambda c: c // side)
    return dot(dot(rows, ones, (1, 0)), columns, (1, 0))


def twice(weight):
    size = weight.shape[0]
    rows = onehot((2 * size, size), lambda r: r % size, same).astype(BF16)
    columns = onehot((size, 2 * size), same, lambda c: c % size).astype(BF16)
    full = dot(dot(rows, weight, (1, 0)).astype(BF16), columns, (1, 0))
    return (full * onehot(full.shape, lambda r: r // size, lambda c: c // size)).astype(BF16)


def kernel(
    seqs, outer,
    signal_hbm, cotangent_hbm, depth_hbm, column_hbm, row_hbm, depth_mask_hbm, column_mask_hbm, row_mask_hbm,
    out_depth, out_column, out_row,
    signal, cotangent, depth_ref, column_ref, row_ref, depth_mask, column_mask, row_mask,
    flipped, send_x, send_g, got_x, got_g, first, mixed, second, wide, back,
    w_row_t, w_depth2, w_column2, sums, land_1, land_2, land_3, land_4, sum_1, sum_2, sum_3,
    load_sem, self_sem, send_sem, recv_sem, part_send, part_recv,
):
    starts = [sum(PARTS[:part]) for part in range(len(PARTS))]
    width = 2 * seqs
    ring = ZL * CORES
    chan, me = lax.axis_index("chan"), lax.axis_index("seq")
    x, z_hi = chan // ZH, chan % ZH
    y, inner = me // ring, me % ring
    z_lo, core = inner // CORES, inner % CORES
    z = z_hi * ZL + z_lo
    local_rows = (outer + MIDDLE) // (X * CORES)

    loads = [
        pltpu.make_async_copy(source, target, load_sem.at[place])
        for place, (source, target) in enumerate((
            (signal_hbm, signal), (cotangent_hbm, cotangent),
            (depth_hbm, depth_ref), (column_hbm, column_ref), (row_hbm, row_ref),
            (depth_mask_hbm, depth_mask), (column_mask_hbm, column_mask), (row_mask_hbm, row_mask),
        ))
    ]
    for load in loads:
        load.start()

    def y_peer(step):
        return chan, lax.rem(y + step, Y) * ring + inner

    def z_peer(step):
        there = lax.rem(z + step, ZH * ZL)
        return x * ZH + there // ZL, y * ring + lax.rem(there, ZL) * CORES + core

    def x_peer(step):
        there = lax.rem(x * CORES + core + step, X * CORES)
        return there // CORES * ZH + z_hi, y * ring + z_lo * CORES + lax.rem(there, CORES)

    barrier = pltpu.get_barrier_semaphore()

    @pl.loop(1, seqs)
    def _(step):
        pl.semaphore_signal(barrier, inc=1, device_id=(chan, lax.rem(me + step, seqs)), device_id_type=MESH)

    greeted = seqs - 1
    for away in range(ZL):
        if ZH == 2:
            pl.semaphore_signal(
                barrier, inc=1,
                device_id=(x * ZH + 1 - z_hi, y * ring + away * CORES + core), device_id_type=MESH,
            )
            greeted += 1
    for step in range(1, X):
        for other in range(CORES):
            there = lax.rem(x + step, X) * ZH + z_hi
            pl.semaphore_signal(
                barrier, inc=1, device_id=(there, y * ring + z_lo * CORES + other), device_id_type=MESH
            )
            greeted += 1

    pick = onehot((seqs, width), same, lambda c: c // 2).astype(BF16)
    even = jnp.where(iota((1, width), 1) % 2 == 0, 1.0, 0.0).astype(BF16)
    odd = jnp.where(iota((1, width), 1) % 2 == 1, 1.0, 0.0).astype(BF16)

    def flip(read, i):
        def body(block, carry):
            value = read(pl.ds(pl.multiple_of(block * INNER, INNER), INNER))
            both = jnp.concatenate([value * even, value * odd], axis=0)
            flipped[pl.ds(pl.multiple_of(block * seqs, seqs), seqs), :] = dot(pick, both, (1, 1))
            return carry

        lax.fori_loop(i * MIDDLE, (i + 1) * MIDDLE, body, 0, unroll=8)

    def column_rows(i, start, count, d):
        return flipped[pl.ds((i * MIDDLE + start) * seqs + d, count, stride=seqs), :]

    def send(pack, buffer, target, start, count, slot):
        rows = pl.ds(start, count)

        def body(turn, carry):
            for place, away in enumerate(Y_ORDER):
                if away >= Y:
                    continue
                step = lax.rem(turn + place + 1, ring)
                to = lax.rem(y + away, Y) * ring + lax.rem(inner + step, ring)
                buffer[to, start : start + count, :] = pack(to).astype(BF16)

                def go():
                    pltpu.make_async_remote_copy(
                        src_ref=buffer.at[to, rows], dst_ref=target.at[me, rows],
                        send_sem=send_sem.at[slot], recv_sem=recv_sem.at[slot],
                        device_id=(chan, to), device_id_type=MESH,
                    ).start()

                if away == 0:
                    pl.when(step != 0)(go)
                else:
                    go()
            return carry

        lax.fori_loop(0, ring, body, 0)
        own = pltpu.make_async_copy(buffer.at[me, rows], target.at[me, rows], self_sem.at[slot])
        own.start()
        return own

    owns = []
    loads[0].wait()
    for i in range(2):
        flip(lambda rows: signal[rows, :], i)
        if i == 0:
            pl.semaphore_wait(barrier, greeted)
        owns.append(
            send(lambda d: column_rows(i, 0, MIDDLE, d), send_x, got_x, i * MIDDLE, MIDDLE, i)
        )

    loads[1].wait()
    for i in range(2):
        flip(lambda rows: (cotangent[rows, :].astype(F32) * signal[rows, :].astype(F32)).astype(BF16), i)
    for part, (start, count) in enumerate(zip(starts, PARTS)):
        def pack_part(d):
            return jnp.concatenate([column_rows(i, start, count, d) for i in range(2)], axis=0)

        owns.append(send(pack_part, send_g, got_g, 2 * start, 2 * count, 2 + part))

    for load in loads[2:]:
        load.wait()
    keep_row = spread_mask(row_mask[...], outer)
    keep_column = spread_mask(column_mask[...], MIDDLE)
    keep_depth = spread_mask(depth_mask[...], INNER)
    w_row = (row_ref[...].astype(F32) * keep_row).astype(BF16)
    w_row_t[...] = dot(onehot((outer, outer), same, same).astype(BF16), w_row, (1, 1)).astype(BF16)
    w_depth2[...] = twice((depth_ref[...].astype(F32) * keep_depth).astype(BF16))
    w_column2[...] = twice((column_ref[...].astype(F32) * keep_column).astype(BF16))

    def arrived(buffer, start, count, slot):
        owns[slot].wait()
        others = buffer.at[pl.ds(0, seqs - 1), pl.ds(start, count)]
        pltpu.make_async_copy(others, others, recv_sem.at[slot]).wait()

    for i in range(2):
        arrived(got_x, i * MIDDLE, MIDDLE, i)

    def signal_side(s, carry):
        field = got_x[s]
        one = dot(field, w_depth2[...], (1, 1)).astype(BF16)
        first[s] = one
        two = dot(w_column2[...], jnp.concatenate([field, one], axis=1), (1, 0))
        for start, count in zip(starts, PARTS):
            mixed[s, 2 * start : 2 * (start + count), :] = jnp.concatenate(
                [two[i * MIDDLE + start : i * MIDDLE + start + count, :LANES] for i in range(2)], axis=0
            ).astype(BF16)
        wide[pl.ds(pl.multiple_of(s * 2 * MIDDLE, 2 * MIDDLE), 2 * MIDDLE), :] = two[:, LANES:]
        return carry

    lax.fori_loop(0, seqs, signal_side, 0, unroll=4)

    def by_column(j, carry):
        second[j] = wide[pl.ds(j, outer, stride=MIDDLE), :].astype(BF16)
        return carry

    lax.fori_loop(0, MIDDLE, by_column, 0, unroll=4)

    grad_row = jnp.zeros((outer, outer), F32)
    grad_depth = jnp.zeros((LANES, LANES), F32)
    group = min(4, seqs)
    for part, (start, count) in enumerate(zip(starts, PARTS)):
        pair = 2 * count
        arrived(got_g, 2 * start, pair, 2 + part)

        def widen(s, carry):
            wide[pl.ds(pl.multiple_of(s * pair, pair), pair), :] = got_g[s, 2 * start : 2 * start + pair, :].astype(F32)
            return carry

        lax.fori_loop(0, seqs, widen, 0, unroll=8)

        def row_side(j, total):
            gated = wide[pl.ds(j, outer, stride=count), :].astype(BF16)
            back[pl.ds(j, outer, stride=count), :] = dot(w_row_t[...], gated, (1, 0))
            return total + dot(gated, second[start + j], (1, 1))

        grad_row = lax.fori_loop(0, count, row_side, grad_row, unroll=4)

        def back_side(block, carry):
            column, depth = carry
            rows = group * pair
            value = back[pl.ds(pl.multiple_of(block * rows, rows), rows), :]
            fields = mixed[pl.ds(block * group, group), 2 * start : 2 * start + pair, :].reshape(rows, LANES)
            depth = depth + dot(value.astype(BF16), fields, (0, 0))
            ours, theirs = [], []
            for s in range(group):
                at = s * pair
                ours.append(jnp.concatenate([value[at : at + count], value[at + count : at + pair]], axis=1))
                one = first[block * group + s]
                theirs.append(jnp.concatenate([one[:MIDDLE], one[MIDDLE:]], axis=1))
            ours = jnp.concatenate(ours, axis=0).astype(BF16)
            column = column + dot(ours, jnp.concatenate(theirs, axis=0), (1, 1))
            return column, depth

        column, grad_depth = lax.fori_loop(
            0, seqs // group, back_side,
            (jnp.zeros((group * count, group * MIDDLE), F32), grad_depth), unroll=2,
        )
        piece = jnp.zeros((count, MIDDLE), F32)
        for s in range(group):
            piece = piece + column[s * count : (s + 1) * count, s * MIDDLE : (s + 1) * MIDDLE]
        sums[outer + start : outer + start + count, :MIDDLE] = piece
    sums[:outer, :outer] = grad_row
    sums[outer:, MIDDLE:] = grad_depth[:INNER, :INNER] + grad_depth[INNER:, INNER:]

    def exchange(phase, count, peer, source, target):
        for step in FAR_FIRST:
            if step < count:
                to = peer(step)
                pltpu.make_async_remote_copy(
                    src_ref=source(to), dst_ref=target,
                    send_sem=part_send.at[phase], recv_sem=part_recv.at[phase],
                    device_id=to, device_id_type=MESH,
                ).start()

    def landed(phase, land, count):
        others = land.at[pl.ds(0, count - 1)]
        pltpu.make_async_copy(others, others, part_recv.at[phase]).wait()

    def added(land):
        total = land[0]
        for slot in range(1, land.shape[0]):
            total = total + land[slot]
        return total

    def rows_of(place):
        return pl.ds(pl.multiple_of(place * local_rows, 8), local_rows)

    def place_of(to):
        return to[0] // ZH * CORES + to[1] % CORES

    place = x * CORES + core
    land_1[place] = sums[rows_of(place), :]
    exchange(0, X * CORES, x_peer, lambda to: sums.at[rows_of(place_of(to))], land_1.at[place])
    landed(0, land_1, X * CORES)
    sum_1[...] = added(land_1)
    land_2[z] = sum_1[...]
    exchange(1, ZH * ZL, z_peer, lambda to: sum_1, land_2.at[z])
    landed(1, land_2, ZH * ZL)
    sum_2[...] = added(land_2)
    land_3[y] = sum_2[...]
    exchange(2, Y, y_peer, lambda to: sum_2, land_3.at[y])
    landed(2, land_3, Y)
    sum_3[...] = added(land_3)
    land_4[place] = sum_3[...]
    exchange(3, X * CORES, x_peer, lambda to: sum_3, land_4.at[place])
    landed(3, land_4, X * CORES)

    whole = land_4[...].reshape(outer + MIDDLE, LANES)
    inner_count = 1.0 / math.sqrt(SEQLEN * CHANNELS // MIDDLE)
    outer_count = 1.0 / math.sqrt(SEQLEN * CHANNELS // outer)
    out_row[...] = jnp.where(keep_row > 0.5, whole[:outer, :outer] * outer_count, 0.0)
    out_column[...] = jnp.where(keep_column > 0.5, whole[outer:, :MIDDLE] * inner_count, 0.0)
    out_depth[...] = jnp.where(keep_depth > 0.5, whole[outer:, MIDDLE:] * inner_count, 0.0)

    def sent(buffer, start, count, slot):
        others = buffer.at[pl.ds(0, seqs - 1), pl.ds(start, count)]
        pltpu.make_async_copy(others, others, send_sem.at[slot]).wait()

    for i in range(2):
        sent(send_x, i * MIDDLE, MIDDLE, i)
    for part, (start, count) in enumerate(zip(starts, PARTS)):
        sent(send_g, 2 * start, 2 * count, 2 + part)
    for phase, (land, count) in enumerate(
        ((land_1, X * CORES), (land_2, ZH * ZL), (land_3, Y), (land_4, X * CORES))
    ):
        others = land.at[pl.ds(0, count - 1)]
        pltpu.make_async_copy(others, others, part_send.at[phase]).wait()


def per_device(
    signal, cotangent, depth_factor, column_factor, row_factor, depth_mask, column_mask, row_mask
):
    seqs = Y * ZL * CORES
    outer = row_factor.shape[0]
    rows, width = signal.shape
    local_rows = (outer + MIDDLE) // (X * CORES)
    vmem = pl.BlockSpec(memory_space=pltpu.VMEM)
    hbm = pl.BlockSpec(memory_space=pltpu.HBM)
    return pl.pallas_call(
        functools.partial(kernel, seqs, outer),
        out_shape=(
            jax.ShapeDtypeStruct((INNER, INNER), F32),
            jax.ShapeDtypeStruct((MIDDLE, MIDDLE), F32),
            jax.ShapeDtypeStruct((outer, outer), F32),
        ),
        in_specs=[hbm] * 8,
        out_specs=(vmem, vmem, vmem),
        scratch_shapes=[
            pltpu.VMEM((rows, width), BF16),
            pltpu.VMEM((rows, width), BF16),
        ] + [
            pltpu.VMEM(a.shape, a.dtype)
            for a in (depth_factor, column_factor, row_factor, depth_mask, column_mask, row_mask)
        ] + [
            pltpu.VMEM((2 * MIDDLE * seqs, LANES), F32),
            pltpu.VMEM((seqs, 2 * MIDDLE, LANES), BF16),
            pltpu.VMEM((seqs, 2 * MIDDLE, LANES), BF16),
            pltpu.VMEM((seqs, 2 * MIDDLE, LANES), BF16),
            pltpu.VMEM((seqs, 2 * MIDDLE, LANES), BF16),
            pltpu.VMEM((seqs, 2 * MIDDLE, LANES), BF16),
            pltpu.VMEM((seqs, 2 * MIDDLE, LANES), BF16),
            pltpu.VMEM((MIDDLE, outer, LANES), BF16),
            pltpu.VMEM((outer * MIDDLE, LANES), F32),
            pltpu.VMEM((outer * max(PARTS), LANES), F32),
            pltpu.VMEM((outer, outer), BF16),
            pltpu.VMEM((LANES, LANES), BF16),
            pltpu.VMEM((LANES, LANES), BF16),
            pltpu.VMEM((outer + MIDDLE, LANES), F32),
            pltpu.VMEM((X * CORES, local_rows, LANES), F32),
            pltpu.VMEM((ZH * ZL, local_rows, LANES), F32),
            pltpu.VMEM((Y, local_rows, LANES), F32),
            pltpu.VMEM((X * CORES, local_rows, LANES), F32),
            pltpu.VMEM((local_rows, LANES), F32),
            pltpu.VMEM((local_rows, LANES), F32),
            pltpu.VMEM((local_rows, LANES), F32),
            pltpu.SemaphoreType.DMA((8,)),
            pltpu.SemaphoreType.DMA((2 + len(PARTS),)),
            pltpu.SemaphoreType.DMA((2 + len(PARTS),)),
            pltpu.SemaphoreType.DMA((2 + len(PARTS),)),
            pltpu.SemaphoreType.DMA((4,)),
            pltpu.SemaphoreType.DMA((4,)),
        ],
        compiler_params=pltpu.CompilerParams(
            collective_id=0, has_side_effects=True, vmem_limit_bytes=60 * 2**20
        ),
        cost_estimate=pl.CostEstimate(flops=1_300_000_000, bytes_accessed=4 * 2**20, transcendentals=0),
    )(signal, cotangent, depth_factor, column_factor, row_factor, depth_mask, column_mask, row_mask)


def solution(mesh):
    in_specs = (P("seq", "chan"), P("seq", "chan"), P(), P(), P(), P(), P(), P())
    out_specs = (P(), P(), P())
    return jax.shard_map(
        per_device, mesh=mesh, in_specs=in_specs, out_specs=out_specs, check_vma=False
    )
```

```python
import functools
import math

import jax
import jax.numpy as jnp
from jax import lax
from jax.experimental import pallas as pl
from jax.experimental.pallas import tpu as pltpu
from jax.sharding import PartitionSpec as P

CHANNELS = 1024
SEQLEN = 524288
MIDDLE = 64
INNER = 64
LANES = 128
X, ZH, Y, ZL, CORES = 4, 2, 8, 4, 2
PARTS = (16, 16, 16, 8, 8)
HEAD = ((0, 0, 16), (0, 16, 48), (1, 0, 64))
Y_ORDER = (1, 7, 2, 6, 3, 5, 4, 0)
FAR_FIRST = (4, 3, 5, 2, 6, 1, 7)
F32, BF16 = jnp.float32, jnp.bfloat16
MESH = pl.DeviceIdType.MESH


def dot(a, b, contract):
    return lax.dot_general(a, b, ((contract[:1], contract[1:]), ((), ())), preferred_element_type=F32)


def iota(shape, axis):
    return lax.broadcasted_iota(jnp.int32, shape, axis)


def onehot(shape, left, right):
    return jnp.where(left(iota(shape, 0)) == right(iota(shape, 1)), 1.0, 0.0)


def same(value):
    return value


def spread_mask(mask, size):
    tiles = mask.shape[0]
    side = size // tiles
    ones = jnp.where(mask == 1, 1.0, 0.0)
    rows = onehot((size, tiles), lambda r: r // side, same)
    columns = onehot((tiles, size), same, lambda c: c // side)
    return dot(dot(rows, ones, (1, 0)), columns, (1, 0))


def twice(weight):
    size = weight.shape[0]
    rows = onehot((2 * size, size), lambda r: r % size, same).astype(BF16)
    columns = onehot((size, 2 * size), same, lambda c: c % size).astype(BF16)
    full = dot(dot(rows, weight, (1, 0)).astype(BF16), columns, (1, 0))
    return (full * onehot(full.shape, lambda r: r // size, lambda c: c // size)).astype(BF16)


def kernel(
    seqs, outer,
    signal_hbm, cotangent_hbm, depth_hbm, column_hbm, row_hbm, depth_mask_hbm, column_mask_hbm, row_mask_hbm,
    out_depth, out_column, out_row,
    signal, cotangent, depth_ref, column_ref, row_ref, depth_mask, column_mask, row_mask,
    flipped, send_x, send_g, got_x, got_g, first_t, mixed_t, second, wide, tall, back,
    w_row_t, w_depth2, w_column2, sums, land_1, land_2, land_3, land_4, sum_1, sum_2, sum_3,
    load_sem, self_sem, send_sem, recv_sem, part_send, part_recv,
):
    starts = [sum(PARTS[:part]) for part in range(len(PARTS))]
    width = 2 * seqs
    ring = ZL * CORES
    chan, me = lax.axis_index("chan"), lax.axis_index("seq")
    x, z_hi = chan // ZH, chan % ZH
    y, inner = me // ring, me % ring
    z_lo, core = inner // CORES, inner % CORES
    z = z_hi * ZL + z_lo
    local_rows = (outer + MIDDLE) // (X * CORES)

    loads = [
        pltpu.make_async_copy(source, target, load_sem.at[place])
        for place, (source, target) in enumerate((
            (signal_hbm, signal), (cotangent_hbm, cotangent),
            (depth_hbm, depth_ref), (column_hbm, column_ref), (row_hbm, row_ref),
            (depth_mask_hbm, depth_mask), (column_mask_hbm, column_mask), (row_mask_hbm, row_mask),
        ))
    ]
    for load in loads:
        load.start()

    def y_peer(step):
        return chan, lax.rem(y + step, Y) * ring + inner

    def z_peer(step):
        there = lax.rem(z + step, ZH * ZL)
        return x * ZH + there // ZL, y * ring + lax.rem(there, ZL) * CORES + core

    def x_peer(step):
        there = lax.rem(x * CORES + core + step, X * CORES)
        return there // CORES * ZH + z_hi, y * ring + z_lo * CORES + lax.rem(there, CORES)

    barrier = pltpu.get_barrier_semaphore()

    @pl.loop(1, seqs)
    def _(step):
        pl.semaphore_signal(barrier, inc=1, device_id=(chan, lax.rem(me + step, seqs)), device_id_type=MESH)

    greeted = seqs - 1
    for away in range(ZL):
        if ZH == 2:
            pl.semaphore_signal(
                barrier, inc=1,
                device_id=(x * ZH + 1 - z_hi, y * ring + away * CORES + core), device_id_type=MESH,
            )
            greeted += 1
    for step in range(1, X):
        for other in range(CORES):
            there = lax.rem(x + step, X) * ZH + z_hi
            pl.semaphore_signal(
                barrier, inc=1, device_id=(there, y * ring + z_lo * CORES + other), device_id_type=MESH
            )
            greeted += 1

    pick = onehot((seqs, width), same, lambda c: c // 2).astype(BF16)
    even = jnp.where(iota((1, width), 1) % 2 == 0, 1.0, 0.0).astype(BF16)
    odd = jnp.where(iota((1, width), 1) % 2 == 1, 1.0, 0.0).astype(BF16)

    def flip(read, i, start, count):
        def body(block, carry):
            value = read(pl.ds(pl.multiple_of(block * 2 * INNER, 2 * INNER), 2 * INNER))
            ones, twos = value * even, value * odd
            both = [ones[:INNER], twos[:INNER], ones[INNER:], twos[INNER:]]
            turned = dot(pick, jnp.concatenate(both, axis=0), (1, 1))
            at = pl.multiple_of(block * 2 * seqs, 2 * seqs)
            flipped[pl.ds(at, seqs), :] = turned[:, :LANES]
            flipped[pl.ds(at + seqs, seqs), :] = turned[:, LANES:]
            return carry

        at = (i * MIDDLE + start) // 2
        lax.fori_loop(at, at + count // 2, body, 0, unroll=8)

    def column_rows(i, start, count, d):
        return flipped[pl.ds((i * MIDDLE + start) * seqs + d, count, stride=seqs), :]

    def send(pack, buffer, target, start, count, slot):
        rows = pl.ds(start, count)

        def body(turn, carry):
            for place, away in enumerate(Y_ORDER):
                if away >= Y:
                    continue
                step = lax.rem(turn + place + 1, ring)
                to = lax.rem(y + away, Y) * ring + lax.rem(inner + step, ring)
                buffer[to, start : start + count, :] = pack(to).astype(BF16)

                def go():
                    pltpu.make_async_remote_copy(
                        src_ref=buffer.at[to, rows], dst_ref=target.at[me, rows],
                        send_sem=send_sem.at[slot], recv_sem=recv_sem.at[slot],
                        device_id=(chan, to), device_id_type=MESH,
                    ).start()

                if away == 0:
                    pl.when(step != 0)(go)
                else:
                    go()
            return carry

        lax.fori_loop(0, ring, body, 0)
        own = pltpu.make_async_copy(buffer.at[me, rows], target.at[me, rows], self_sem.at[slot])
        own.start()
        return own

    owns = []
    loads[0].wait()
    for part, (i, start, count) in enumerate(HEAD):
        flip(lambda rows: signal[rows, :], i, start, count)
        if part == 0:
            pl.semaphore_wait(barrier, greeted)
        owns.append(send(
            lambda d: column_rows(i, start, count, d), send_x, got_x, i * MIDDLE + start, count, part
        ))

    loads[1].wait()
    for i in range(2):
        flip(
            lambda rows: (cotangent[rows, :].astype(F32) * signal[rows, :].astype(F32)).astype(BF16),
            i, 0, MIDDLE,
        )
    for part, (start, count) in enumerate(zip(starts, PARTS)):
        def pack_part(d):
            return jnp.concatenate([column_rows(i, start, count, d) for i in range(2)], axis=0)

        owns.append(send(pack_part, send_g, got_g, 2 * start, 2 * count, len(HEAD) + part))

    for load in loads[2:]:
        load.wait()
    keep_row = spread_mask(row_mask[...], outer)
    keep_column = spread_mask(column_mask[...], MIDDLE)
    keep_depth = spread_mask(depth_mask[...], INNER)
    w_row = (row_ref[...].astype(F32) * keep_row).astype(BF16)
    w_row_t[...] = dot(onehot((outer, outer), same, same).astype(BF16), w_row, (1, 1)).astype(BF16)
    w_depth2[...] = twice((depth_ref[...].astype(F32) * keep_depth).astype(BF16))
    w_column2[...] = twice((column_ref[...].astype(F32) * keep_column).astype(BF16))

    def arrived(buffer, start, count, slot):
        owns[slot].wait()
        others = buffer.at[pl.ds(0, seqs - 1), pl.ds(start, count)]
        pltpu.make_async_copy(others, others, recv_sem.at[slot]).wait()

    for part, (i, start, count) in enumerate(HEAD):
        arrived(got_x, i * MIDDLE + start, count, part)

    def signal_side(s, carry):
        field = got_x[s]
        first = dot(field, w_depth2[...], (1, 1)).astype(BF16)
        first_t[pl.ds(pl.multiple_of(s * LANES, LANES), LANES), :] = dot(w_depth2[...], field, (1, 1)).astype(BF16)
        both = dot(w_column2[...], jnp.concatenate([field, first], axis=1), (1, 0))
        rows = pl.ds(pl.multiple_of(s * 2 * MIDDLE, 2 * MIDDLE), 2 * MIDDLE)
        tall[rows, :] = both[:, :LANES]
        wide[rows, :] = both[:, LANES:]
        return carry

    lax.fori_loop(0, seqs, signal_side, 0, unroll=4)

    same_lane = onehot((LANES, LANES), same, same).astype(BF16)

    def by_column(two, carry):
        at = [pl.ds(2 * two + j, outer, stride=MIDDLE) for j in range(2)]
        second[two] = jnp.concatenate([wide[rows, :] for rows in at], axis=1).astype(BF16)
        mixed = jnp.concatenate([tall[rows, :] for rows in at], axis=0).astype(BF16)
        mixed_t[two] = dot(same_lane, mixed, (1, 1)).astype(BF16)
        return carry

    lax.fori_loop(0, MIDDLE // 2, by_column, 0, unroll=4)

    grad_row = jnp.zeros((outer, outer), F32)
    grad_depth_t = jnp.zeros((LANES, LANES), F32)
    for part, (start, count) in enumerate(zip(starts, PARTS)):
        pair = 2 * count
        arrived(got_g, 2 * start, pair, len(HEAD) + part)

        def widen(s, carry):
            wide[pl.ds(pl.multiple_of(s * pair, pair), pair), :] = got_g[s, 2 * start : 2 * start + pair, :].astype(F32)
            return carry

        lax.fori_loop(0, seqs, widen, 0, unroll=16 if seqs % 16 == 0 else 1)

        def column_side(two, carry):
            row, depth_t = carry
            at = [pl.ds(2 * two + j, outer, stride=count) for j in range(2)]
            gated = jnp.concatenate([wide[rows, :] for rows in at], axis=1).astype(BF16)
            value = dot(w_row_t[...], gated, (1, 0))
            for j in range(2):
                back[at[j], :] = value[:, j * LANES : (j + 1) * LANES]
            value = value.astype(BF16)
            value = jnp.concatenate([value[:, :LANES], value[:, LANES:]], axis=0)
            row = row + dot(gated, second[start // 2 + two], (1, 1))
            depth_t = depth_t + dot(mixed_t[start // 2 + two], value, (1, 0))
            return row, depth_t

        grad_row, grad_depth_t = lax.fori_loop(
            0, count // 2, column_side, (grad_row, grad_depth_t), unroll=2
        )

        def back_side(two, column):
            rows = [pl.ds(pl.multiple_of((2 * two + s) * pair, pair), pair) for s in range(2)]
            value = jnp.concatenate([back[at, :] for at in rows], axis=1).astype(BF16)
            return column + dot(value, first_t[pl.ds(pl.multiple_of(two * 2 * LANES, 2 * LANES), 2 * LANES), :], (1, 0))

        column = lax.fori_loop(
            0, seqs // 2, back_side, jnp.zeros((pair, LANES), F32), unroll=min(8, seqs // 4)
        )
        sums[outer + start : outer + start + count, :MIDDLE] = column[:count, :MIDDLE] + column[count:, MIDDLE:]
    sums[:outer, :outer] = grad_row
    sums[outer:, MIDDLE:] = grad_depth_t[:INNER, :INNER] + grad_depth_t[INNER:, INNER:]

    def exchange(phase, count, peer, source, target):
        for step in FAR_FIRST:
            if step < count:
                to = peer(step)
                pltpu.make_async_remote_copy(
                    src_ref=source(to), dst_ref=target,
                    send_sem=part_send.at[phase], recv_sem=part_recv.at[phase],
                    device_id=to, device_id_type=MESH,
                ).start()

    def landed(phase, land, count):
        others = land.at[pl.ds(0, count - 1)]
        pltpu.make_async_copy(others, others, part_recv.at[phase]).wait()

    def added(land):
        total = land[0]
        for slot in range(1, land.shape[0]):
            total = total + land[slot]
        return total

    def rows_of(place):
        return pl.ds(pl.multiple_of(place * local_rows, 8), local_rows)

    def place_of(to):
        return to[0] // ZH * CORES + to[1] % CORES

    place = x * CORES + core
    land_1[place] = sums[rows_of(place), :]
    exchange(0, X * CORES, x_peer, lambda to: sums.at[rows_of(place_of(to))], land_1.at[place])
    landed(0, land_1, X * CORES)
    sum_1[...] = added(land_1)
    land_2[z] = sum_1[...]
    exchange(1, ZH * ZL, z_peer, lambda to: sum_1, land_2.at[z])
    landed(1, land_2, ZH * ZL)
    sum_2[...] = added(land_2)
    land_3[y] = sum_2[...]
    exchange(2, Y, y_peer, lambda to: sum_2, land_3.at[y])
    landed(2, land_3, Y)
    sum_3[...] = added(land_3)
    land_4[place] = sum_3[...]
    exchange(3, X * CORES, x_peer, lambda to: sum_3, land_4.at[place])
    landed(3, land_4, X * CORES)

    whole = land_4[...].reshape(outer + MIDDLE, LANES)
    inner_count = 1.0 / math.sqrt(SEQLEN * CHANNELS // MIDDLE)
    outer_count = 1.0 / math.sqrt(SEQLEN * CHANNELS // outer)
    out_row[...] = jnp.where(keep_row > 0.5, whole[:outer, :outer] * outer_count, 0.0)
    out_column[...] = jnp.where(keep_column > 0.5, whole[outer:, :MIDDLE] * inner_count, 0.0)
    out_depth[...] = jnp.where(keep_depth > 0.5, whole[outer:, MIDDLE:].T * inner_count, 0.0)

    def sent(buffer, start, count, slot):
        others = buffer.at[pl.ds(0, seqs - 1), pl.ds(start, count)]
        pltpu.make_async_copy(others, others, send_sem.at[slot]).wait()

    for part, (i, start, count) in enumerate(HEAD):
        sent(send_x, i * MIDDLE + start, count, part)
    for part, (start, count) in enumerate(zip(starts, PARTS)):
        sent(send_g, 2 * start, 2 * count, len(HEAD) + part)
    for phase, (land, count) in enumerate(
        ((land_1, X * CORES), (land_2, ZH * ZL), (land_3, Y), (land_4, X * CORES))
    ):
        others = land.at[pl.ds(0, count - 1)]
        pltpu.make_async_copy(others, others, part_send.at[phase]).wait()


def hand_over(*refs):
    sources, targets, sem = refs[:3], refs[3:6], refs[6]
    copies = [
        pltpu.make_async_copy(source, target, sem.at[place])
        for place, (source, target) in enumerate(zip(sources, targets))
    ]
    for copy in copies:
        copy.start()
    for copy in copies:
        copy.wait()


def per_device(
    signal, cotangent, depth_factor, column_factor, row_factor, depth_mask, column_mask, row_mask
):
    seqs = Y * ZL * CORES
    outer = row_factor.shape[0]
    rows, width = signal.shape
    local_rows = (outer + MIDDLE) // (X * CORES)
    vmem = pl.BlockSpec(memory_space=pltpu.VMEM)
    hbm = pl.BlockSpec(memory_space=pltpu.HBM)
    shapes = (
        jax.ShapeDtypeStruct((INNER, INNER), F32),
        jax.ShapeDtypeStruct((MIDDLE, MIDDLE), F32),
        jax.ShapeDtypeStruct((outer, outer), F32),
    )
    results = pl.pallas_call(
        functools.partial(kernel, seqs, outer),
        out_shape=shapes,
        in_specs=[hbm] * 8,
        out_specs=(vmem, vmem, vmem),
        scratch_shapes=[
            pltpu.VMEM((rows, width), BF16),
            pltpu.VMEM((rows, width), BF16),
        ] + [
            pltpu.VMEM(a.shape, a.dtype)
            for a in (depth_factor, column_factor, row_factor, depth_mask, column_mask, row_mask)
        ] + [
            pltpu.VMEM((2 * MIDDLE * seqs, LANES), F32),
            pltpu.VMEM((seqs, 2 * MIDDLE, LANES), BF16),
            pltpu.VMEM((seqs, 2 * MIDDLE, LANES), BF16),
            pltpu.VMEM((seqs, 2 * MIDDLE, LANES), BF16),
            pltpu.VMEM((seqs, 2 * MIDDLE, LANES), BF16),
            pltpu.VMEM((seqs * LANES, 2 * MIDDLE), BF16),
            pltpu.VMEM((MIDDLE // 2, LANES, 2 * outer), BF16),
            pltpu.VMEM((MIDDLE // 2, outer, 2 * LANES), BF16),
            pltpu.VMEM((outer * MIDDLE, LANES), F32),
            pltpu.VMEM((outer * MIDDLE, LANES), F32),
            pltpu.VMEM((outer * max(PARTS), LANES), F32),
            pltpu.VMEM((outer, outer), BF16),
            pltpu.VMEM((LANES, LANES), BF16),
            pltpu.VMEM((LANES, LANES), BF16),
            pltpu.VMEM((outer + MIDDLE, LANES), F32),
            pltpu.VMEM((X * CORES, local_rows, LANES), F32),
            pltpu.VMEM((ZH * ZL, local_rows, LANES), F32),
            pltpu.VMEM((Y, local_rows, LANES), F32),
            pltpu.VMEM((X * CORES, local_rows, LANES), F32),
            pltpu.VMEM((local_rows, LANES), F32),
            pltpu.VMEM((local_rows, LANES), F32),
            pltpu.VMEM((local_rows, LANES), F32),
            pltpu.SemaphoreType.DMA((8,)),
            pltpu.SemaphoreType.DMA((len(HEAD) + len(PARTS),)),
            pltpu.SemaphoreType.DMA((len(HEAD) + len(PARTS),)),
            pltpu.SemaphoreType.DMA((len(HEAD) + len(PARTS),)),
            pltpu.SemaphoreType.DMA((4,)),
            pltpu.SemaphoreType.DMA((4,)),
        ],
        compiler_params=pltpu.CompilerParams(
            collective_id=0, has_side_effects=True, vmem_limit_bytes=60 * 2**20
        ),
        cost_estimate=pl.CostEstimate(flops=1_300_000_000, bytes_accessed=4 * 2**20, transcendentals=0),
    )(signal, cotangent, depth_factor, column_factor, row_factor, depth_mask, column_mask, row_mask)
    return pl.pallas_call(
        hand_over,
        out_shape=shapes,
        in_specs=[hbm] * 3,
        out_specs=(hbm, hbm, hbm),
        scratch_shapes=[pltpu.SemaphoreType.DMA((3,))],
        compiler_params=pltpu.CompilerParams(vmem_limit_bytes=60 * 2**20),
    )(*results)


def solution(mesh):
    in_specs = (P("seq", "chan"), P("seq", "chan"), P(), P(), P(), P(), P(), P())
    out_specs = (P(), P(), P())
    return jax.shard_map(
        per_device, mesh=mesh, in_specs=in_specs, out_specs=out_specs, check_vma=False
    )
```

```python
import functools
import math

import jax
import jax.numpy as jnp
from jax import lax
from jax.experimental import pallas as pl
from jax.experimental.pallas import tpu as pltpu
from jax.sharding import PartitionSpec as P

CHANNELS = 1024
SEQLEN = 524288
MIDDLE = 64
INNER = 64
LANES = 128
X, ZH, Y, ZL, CORES = 4, 2, 8, 4, 2
PARTS = (16, 16, 16, 8, 8)
HEAD = ((0, 0, 16), (0, 16, 48), (1, 0, 64))
Y_ORDER = (1, 7, 2, 6, 3, 5, 4, 0)
FAR_FIRST = (4, 3, 5, 2, 6, 1, 7)
F32, BF16 = jnp.float32, jnp.bfloat16
MESH = pl.DeviceIdType.MESH


def dot(a, b, contract):
    return lax.dot_general(a, b, ((contract[:1], contract[1:]), ((), ())), preferred_element_type=F32)


def iota(shape, axis):
    return lax.broadcasted_iota(jnp.int32, shape, axis)


def onehot(shape, left, right):
    return jnp.where(left(iota(shape, 0)) == right(iota(shape, 1)), 1.0, 0.0)


def same(value):
    return value


def spread_mask(mask, size):
    tiles = mask.shape[0]
    side = size // tiles
    ones = jnp.where(mask == 1, 1.0, 0.0)
    rows = onehot((size, tiles), lambda r: r // side, same)
    columns = onehot((tiles, size), same, lambda c: c // side)
    return dot(dot(rows, ones, (1, 0)), columns, (1, 0))


def twice(weight):
    size = weight.shape[0]
    rows = onehot((2 * size, size), lambda r: r % size, same).astype(BF16)
    columns = onehot((size, 2 * size), same, lambda c: c % size).astype(BF16)
    full = dot(dot(rows, weight, (1, 0)).astype(BF16), columns, (1, 0))
    return (full * onehot(full.shape, lambda r: r // size, lambda c: c // size)).astype(BF16)


def kernel(
    seqs, outer,
    signal_hbm, cotangent_hbm, depth_hbm, column_hbm, row_hbm, depth_mask_hbm, column_mask_hbm, row_mask_hbm,
    out_depth, out_column, out_row,
    signal, cotangent, depth_ref, column_ref, row_ref, depth_mask, column_mask, row_mask,
    flipped, send_x, send_g, got_x, got_g, first_t, mixed_t, second, wide, tall, back,
    w_row_t, w_depth2, w_column2, sums, land_1, land_2, land_3, land_4, sum_1, sum_2, sum_3,
    load_sem, self_sem, send_sem, recv_sem, part_send, part_recv,
):
    starts = [sum(PARTS[:part]) for part in range(len(PARTS))]
    width = 2 * seqs
    ring = ZL * CORES
    chan, me = lax.axis_index("chan"), lax.axis_index("seq")
    x, z_hi = chan // ZH, chan % ZH
    y, inner = me // ring, me % ring
    z_lo, core = inner // CORES, inner % CORES
    z = z_hi * ZL + z_lo
    local_rows = (outer + MIDDLE) // (X * CORES)

    loads = [
        pltpu.make_async_copy(source, target, load_sem.at[place])
        for place, (source, target) in enumerate((
            (signal_hbm, signal), (cotangent_hbm, cotangent),
            (depth_hbm, depth_ref), (column_hbm, column_ref), (row_hbm, row_ref),
            (depth_mask_hbm, depth_mask), (column_mask_hbm, column_mask), (row_mask_hbm, row_mask),
        ))
    ]
    for load in loads:
        load.start()

    def y_peer(step):
        return chan, lax.rem(y + step, Y) * ring + inner

    def z_peer(step):
        there = lax.rem(z + step, ZH * ZL)
        return x * ZH + there // ZL, y * ring + lax.rem(there, ZL) * CORES + core

    def x_peer(step):
        there = lax.rem(x * CORES + core + step, X * CORES)
        return there // CORES * ZH + z_hi, y * ring + z_lo * CORES + lax.rem(there, CORES)

    barrier = pltpu.get_barrier_semaphore()

    @pl.loop(0, seqs - 1)
    def _(turn):
        step = 1 + lax.rem(turn + seqs // 2 - ring // 2, seqs - 1)
        pl.semaphore_signal(barrier, inc=1, device_id=(chan, lax.rem(me + step, seqs)), device_id_type=MESH)

    greeted = seqs - 1
    for away in range(ZL):
        if ZH == 2:
            pl.semaphore_signal(
                barrier, inc=1,
                device_id=(x * ZH + 1 - z_hi, y * ring + away * CORES + core), device_id_type=MESH,
            )
            greeted += 1
    for step in range(1, X):
        for other in range(CORES):
            there = lax.rem(x + step, X) * ZH + z_hi
            pl.semaphore_signal(
                barrier, inc=1, device_id=(there, y * ring + z_lo * CORES + other), device_id_type=MESH
            )
            greeted += 1

    pick = onehot((seqs, width), same, lambda c: c // 2).astype(BF16)
    even = jnp.where(iota((1, width), 1) % 2 == 0, 1.0, 0.0).astype(BF16)
    odd = jnp.where(iota((1, width), 1) % 2 == 1, 1.0, 0.0).astype(BF16)

    def flip(read, i, start, count):
        def body(block, carry):
            value = read(pl.ds(pl.multiple_of(block * 2 * INNER, 2 * INNER), 2 * INNER))
            ones, twos = value * even, value * odd
            both = [ones[:INNER], twos[:INNER], ones[INNER:], twos[INNER:]]
            turned = dot(pick, jnp.concatenate(both, axis=0), (1, 1))
            at = pl.multiple_of(block * 2 * seqs, 2 * seqs)
            flipped[pl.ds(at, seqs), :] = turned[:, :LANES]
            flipped[pl.ds(at + seqs, seqs), :] = turned[:, LANES:]
            return carry

        at = (i * MIDDLE + start) // 2
        lax.fori_loop(at, at + count // 2, body, 0, unroll=8)

    def column_rows(i, start, count, d):
        return flipped[pl.ds((i * MIDDLE + start) * seqs + d, count, stride=seqs), :]

    def send(pack, buffer, target, start, count, slot):
        rows = pl.ds(start, count)

        def body(turn, carry):
            for place, away in enumerate(Y_ORDER):
                if away >= Y:
                    continue
                step = lax.rem(turn + place + 1, ring)
                to = lax.rem(y + away, Y) * ring + lax.rem(inner + step, ring)
                buffer[to, start : start + count, :] = pack(to).astype(BF16)

                def go():
                    pltpu.make_async_remote_copy(
                        src_ref=buffer.at[to, rows], dst_ref=target.at[me, rows],
                        send_sem=send_sem.at[slot], recv_sem=recv_sem.at[slot],
                        device_id=(chan, to), device_id_type=MESH,
                    ).start()

                if away == 0:
                    pl.when(step != 0)(go)
                else:
                    go()
            return carry

        lax.fori_loop(0, ring, body, 0)
        own = pltpu.make_async_copy(buffer.at[me, rows], target.at[me, rows], self_sem.at[slot])
        own.start()
        return own

    owns = []
    loads[0].wait()
    for part, (i, start, count) in enumerate(HEAD):
        flip(lambda rows: signal[rows, :], i, start, count)
        if part == 0:
            pl.semaphore_wait(barrier, greeted)
        owns.append(send(
            lambda d: column_rows(i, start, count, d), send_x, got_x, i * MIDDLE + start, count, part
        ))

    loads[1].wait()
    for i in range(2):
        flip(
            lambda rows: (cotangent[rows, :].astype(F32) * signal[rows, :].astype(F32)).astype(BF16),
            i, 0, MIDDLE,
        )
    for part, (start, count) in enumerate(zip(starts, PARTS)):
        def pack_part(d):
            return jnp.concatenate([column_rows(i, start, count, d) for i in range(2)], axis=0)

        owns.append(send(pack_part, send_g, got_g, 2 * start, 2 * count, len(HEAD) + part))

    for load in loads[2:]:
        load.wait()
    keep_row = spread_mask(row_mask[...], outer)
    keep_column = spread_mask(column_mask[...], MIDDLE)
    keep_depth = spread_mask(depth_mask[...], INNER)
    w_row = (row_ref[...].astype(F32) * keep_row).astype(BF16)
    w_row_t[...] = dot(onehot((outer, outer), same, same).astype(BF16), w_row, (1, 1)).astype(BF16)
    w_depth2[...] = twice((depth_ref[...].astype(F32) * keep_depth).astype(BF16))
    w_column2[...] = twice((column_ref[...].astype(F32) * keep_column).astype(BF16))

    def arrived(buffer, start, count, slot):
        owns[slot].wait()
        others = buffer.at[pl.ds(0, seqs - 1), pl.ds(start, count)]
        pltpu.make_async_copy(others, others, recv_sem.at[slot]).wait()

    for part, (i, start, count) in enumerate(HEAD):
        arrived(got_x, i * MIDDLE + start, count, part)

    def signal_side(s, carry):
        field = got_x[s]
        first = dot(field, w_depth2[...], (1, 1)).astype(BF16)
        first_t[pl.ds(pl.multiple_of(s * LANES, LANES), LANES), :] = dot(w_depth2[...], field, (1, 1)).astype(BF16)
        both = dot(w_column2[...], jnp.concatenate([field, first], axis=1), (1, 0))
        rows = pl.ds(pl.multiple_of(s * 2 * MIDDLE, 2 * MIDDLE), 2 * MIDDLE)
        tall[rows, :] = both[:, :LANES]
        wide[rows, :] = both[:, LANES:]
        return carry

    lax.fori_loop(0, seqs, signal_side, 0, unroll=4)

    same_lane = onehot((LANES, LANES), same, same).astype(BF16)

    def by_column(two, carry):
        at = [pl.ds(2 * two + j, outer, stride=MIDDLE) for j in range(2)]
        second[two] = jnp.concatenate([wide[rows, :] for rows in at], axis=1).astype(BF16)
        mixed = jnp.concatenate([tall[rows, :] for rows in at], axis=0).astype(BF16)
        mixed_t[two] = dot(same_lane, mixed, (1, 1)).astype(BF16)
        return carry

    lax.fori_loop(0, MIDDLE // 2, by_column, 0, unroll=4)

    grad_row = jnp.zeros((outer, outer), F32)
    grad_depth_t = jnp.zeros((LANES, LANES), F32)
    for part, (start, count) in enumerate(zip(starts, PARTS)):
        pair = 2 * count
        arrived(got_g, 2 * start, pair, len(HEAD) + part)

        def widen(s, carry):
            wide[pl.ds(pl.multiple_of(s * pair, pair), pair), :] = got_g[s, 2 * start : 2 * start + pair, :].astype(F32)
            return carry

        lax.fori_loop(0, seqs, widen, 0, unroll=16 if seqs % 16 == 0 else 1)

        def column_side(two, carry):
            row, depth_t = carry
            at = [pl.ds(2 * two + j, outer, stride=count) for j in range(2)]
            gated = jnp.concatenate([wide[rows, :] for rows in at], axis=1).astype(BF16)
            value = dot(w_row_t[...], gated, (1, 0))
            for j in range(2):
                back[at[j], :] = value[:, j * LANES : (j + 1) * LANES]
            value = value.astype(BF16)
            value = jnp.concatenate([value[:, :LANES], value[:, LANES:]], axis=0)
            row = row + dot(gated, second[start // 2 + two], (1, 1))
            depth_t = depth_t + dot(mixed_t[start // 2 + two], value, (1, 0))
            return row, depth_t

        grad_row, grad_depth_t = lax.fori_loop(
            0, count // 2, column_side, (grad_row, grad_depth_t), unroll=2
        )

        def back_side(two, column):
            rows = [pl.ds(pl.multiple_of((2 * two + s) * pair, pair), pair) for s in range(2)]
            value = jnp.concatenate([back[at, :] for at in rows], axis=1).astype(BF16)
            return column + dot(value, first_t[pl.ds(pl.multiple_of(two * 2 * LANES, 2 * LANES), 2 * LANES), :], (1, 0))

        column = lax.fori_loop(
            0, seqs // 2, back_side, jnp.zeros((pair, LANES), F32), unroll=min(8, seqs // 4)
        )
        sums[outer + start : outer + start + count, :MIDDLE] = column[:count, :MIDDLE] + column[count:, MIDDLE:]
    sums[:outer, :outer] = grad_row
    sums[outer:, MIDDLE:] = grad_depth_t[:INNER, :INNER] + grad_depth_t[INNER:, INNER:]

    def exchange(phase, count, peer, source, target):
        for step in FAR_FIRST:
            if step < count:
                to = peer(step)
                pltpu.make_async_remote_copy(
                    src_ref=source(to), dst_ref=target,
                    send_sem=part_send.at[phase], recv_sem=part_recv.at[phase],
                    device_id=to, device_id_type=MESH,
                ).start()

    def landed(phase, land, count):
        others = land.at[pl.ds(0, count - 1)]
        pltpu.make_async_copy(others, others, part_recv.at[phase]).wait()

    def added(land):
        total = land[0]
        for slot in range(1, land.shape[0]):
            total = total + land[slot]
        return total

    def rows_of(place):
        return pl.ds(pl.multiple_of(place * local_rows, 8), local_rows)

    def place_of(to):
        return to[0] // ZH * CORES + to[1] % CORES

    place = x * CORES + core
    land_1[place] = sums[rows_of(place), :]
    exchange(0, X * CORES, x_peer, lambda to: sums.at[rows_of(place_of(to))], land_1.at[place])
    landed(0, land_1, X * CORES)
    sum_1[...] = added(land_1)
    land_2[z] = sum_1[...]
    exchange(1, ZH * ZL, z_peer, lambda to: sum_1, land_2.at[z])
    landed(1, land_2, ZH * ZL)
    sum_2[...] = added(land_2)
    land_3[y] = sum_2[...]
    exchange(2, Y, y_peer, lambda to: sum_2, land_3.at[y])
    landed(2, land_3, Y)
    sum_3[...] = added(land_3)
    land_4[place] = sum_3[...]
    exchange(3, X * CORES, x_peer, lambda to: sum_3, land_4.at[place])
    landed(3, land_4, X * CORES)

    whole = land_4[...].reshape(outer + MIDDLE, LANES)
    inner_count = 1.0 / math.sqrt(SEQLEN * CHANNELS // MIDDLE)
    outer_count = 1.0 / math.sqrt(SEQLEN * CHANNELS // outer)
    out_row[...] = jnp.where(keep_row > 0.5, whole[:outer, :outer] * outer_count, 0.0)
    out_column[...] = jnp.where(keep_column > 0.5, whole[outer:, :MIDDLE] * inner_count, 0.0)
    out_depth[...] = jnp.where(keep_depth > 0.5, whole[outer:, MIDDLE:].T * inner_count, 0.0)

    def sent(buffer, start, count, slot):
        others = buffer.at[pl.ds(0, seqs - 1), pl.ds(start, count)]
        pltpu.make_async_copy(others, others, send_sem.at[slot]).wait()

    for part, (i, start, count) in enumerate(HEAD):
        sent(send_x, i * MIDDLE + start, count, part)
    for part, (start, count) in enumerate(zip(starts, PARTS)):
        sent(send_g, 2 * start, 2 * count, len(HEAD) + part)
    for phase, (land, count) in enumerate(
        ((land_1, X * CORES), (land_2, ZH * ZL), (land_3, Y), (land_4, X * CORES))
    ):
        others = land.at[pl.ds(0, count - 1)]
        pltpu.make_async_copy(others, others, part_send.at[phase]).wait()


def hand_over(*refs):
    sources, targets, held, sem = refs[:3], refs[3:6], refs[6:9], refs[9]
    loads = [
        pltpu.make_async_copy(source, place, sem.at[i])
        for i, (source, place) in enumerate(zip(sources, held))
    ]
    stores = [
        pltpu.make_async_copy(place, target, sem.at[3 + i])
        for i, (place, target) in enumerate(zip(held, targets))
    ]
    for load in loads:
        load.start()
    for load, store in zip(loads, stores):
        load.wait()
        store.start()
    for store in stores:
        store.wait()


def per_device(
    signal, cotangent, depth_factor, column_factor, row_factor, depth_mask, column_mask, row_mask
):
    seqs = Y * ZL * CORES
    outer = row_factor.shape[0]
    rows, width = signal.shape
    local_rows = (outer + MIDDLE) // (X * CORES)
    vmem = pl.BlockSpec(memory_space=pltpu.VMEM)
    hbm = pl.BlockSpec(memory_space=pltpu.HBM)
    shapes = (
        jax.ShapeDtypeStruct((INNER, INNER), F32),
        jax.ShapeDtypeStruct((MIDDLE, MIDDLE), F32),
        jax.ShapeDtypeStruct((outer, outer), F32),
    )
    results = pl.pallas_call(
        functools.partial(kernel, seqs, outer),
        out_shape=shapes,
        in_specs=[hbm] * 8,
        out_specs=(vmem, vmem, vmem),
        scratch_shapes=[
            pltpu.VMEM((rows, width), BF16),
            pltpu.VMEM((rows, width), BF16),
        ] + [
            pltpu.VMEM(a.shape, a.dtype)
            for a in (depth_factor, column_factor, row_factor, depth_mask, column_mask, row_mask)
        ] + [
            pltpu.VMEM((2 * MIDDLE * seqs, LANES), F32),
            pltpu.VMEM((seqs, 2 * MIDDLE, LANES), BF16),
            pltpu.VMEM((seqs, 2 * MIDDLE, LANES), BF16),
            pltpu.VMEM((seqs, 2 * MIDDLE, LANES), BF16),
            pltpu.VMEM((seqs, 2 * MIDDLE, LANES), BF16),
            pltpu.VMEM((seqs * LANES, 2 * MIDDLE), BF16),
            pltpu.VMEM((MIDDLE // 2, LANES, 2 * outer), BF16),
            pltpu.VMEM((MIDDLE // 2, outer, 2 * LANES), BF16),
            pltpu.VMEM((outer * MIDDLE, LANES), F32),
            pltpu.VMEM((outer * MIDDLE, LANES), F32),
            pltpu.VMEM((outer * max(PARTS), LANES), F32),
            pltpu.VMEM((outer, outer), BF16),
            pltpu.VMEM((LANES, LANES), BF16),
            pltpu.VMEM((LANES, LANES), BF16),
            pltpu.VMEM((outer + MIDDLE, LANES), F32),
            pltpu.VMEM((X * CORES, local_rows, LANES), F32),
            pltpu.VMEM((ZH * ZL, local_rows, LANES), F32),
            pltpu.VMEM((Y, local_rows, LANES), F32),
            pltpu.VMEM((X * CORES, local_rows, LANES), F32),
            pltpu.VMEM((local_rows, LANES), F32),
            pltpu.VMEM((local_rows, LANES), F32),
            pltpu.VMEM((local_rows, LANES), F32),
            pltpu.SemaphoreType.DMA((8,)),
            pltpu.SemaphoreType.DMA((len(HEAD) + len(PARTS),)),
            pltpu.SemaphoreType.DMA((len(HEAD) + len(PARTS),)),
            pltpu.SemaphoreType.DMA((len(HEAD) + len(PARTS),)),
            pltpu.SemaphoreType.DMA((4,)),
            pltpu.SemaphoreType.DMA((4,)),
        ],
        compiler_params=pltpu.CompilerParams(
            collective_id=0, has_side_effects=True, vmem_limit_bytes=60 * 2**20
        ),
        cost_estimate=pl.CostEstimate(flops=1_300_000_000, bytes_accessed=4 * 2**20, transcendentals=0),
    )(signal, cotangent, depth_factor, column_factor, row_factor, depth_mask, column_mask, row_mask)
    return pl.pallas_call(
        hand_over,
        out_shape=shapes,
        in_specs=[hbm] * 3,
        out_specs=(hbm, hbm, hbm),
        scratch_shapes=[pltpu.VMEM(a.shape, a.dtype) for a in shapes] + [pltpu.SemaphoreType.DMA((6,))],
        compiler_params=pltpu.CompilerParams(vmem_limit_bytes=60 * 2**20),
    )(*results)


def solution(mesh):
    in_specs = (P("seq", "chan"), P("seq", "chan"), P(), P(), P(), P(), P(), P())
    out_specs = (P(), P(), P())
    return jax.shard_map(
        per_device, mesh=mesh, in_specs=in_specs, out_specs=out_specs, check_vma=False
    )
```

```python
import functools
import math

import jax
import jax.numpy as jnp
from jax import lax
from jax.experimental import pallas as pl
from jax.experimental.pallas import tpu as pltpu
from jax.sharding import PartitionSpec as P

CHANNELS = 1024
SEQLEN = 524288
MIDDLE = 64
INNER = 64
LANES = 128
X, ZH, Y, ZL, CORES = 4, 2, 8, 4, 2
PARTS = (16, 16, 16, 8, 8)
HEAD = ((0, 0, 16), (0, 16, 48), (1, 0, 64))
Y_ORDER = (1, 7, 2, 6, 3, 5, 4, 0)
FAR_FIRST = (4, 3, 5, 2, 6, 1, 7)
F32, BF16 = jnp.float32, jnp.bfloat16
MESH = pl.DeviceIdType.MESH


def dot(a, b, contract):
    return lax.dot_general(a, b, ((contract[:1], contract[1:]), ((), ())), preferred_element_type=F32)


def iota(shape, axis):
    return lax.broadcasted_iota(jnp.int32, shape, axis)


def onehot(shape, left, right):
    return jnp.where(left(iota(shape, 0)) == right(iota(shape, 1)), 1.0, 0.0)


def same(value):
    return value


def spread_mask(mask, size):
    tiles = mask.shape[0]
    side = size // tiles
    ones = jnp.where(mask == 1, 1.0, 0.0)
    rows = onehot((size, tiles), lambda r: r // side, same)
    columns = onehot((tiles, size), same, lambda c: c // side)
    return dot(dot(rows, ones, (1, 0)), columns, (1, 0))


def twice(weight):
    size = weight.shape[0]
    rows = onehot((2 * size, size), lambda r: r % size, same).astype(BF16)
    columns = onehot((size, 2 * size), same, lambda c: c % size).astype(BF16)
    full = dot(dot(rows, weight, (1, 0)).astype(BF16), columns, (1, 0))
    return (full * onehot(full.shape, lambda r: r // size, lambda c: c // size)).astype(BF16)


def kernel(
    seqs, outer,
    signal_hbm, cotangent_hbm, depth_hbm, column_hbm, row_hbm, depth_mask_hbm, column_mask_hbm, row_mask_hbm,
    out_depth, out_column, out_row,
    signal, cotangent, depth_ref, column_ref, row_ref, depth_mask, column_mask, row_mask,
    flipped, send_x, send_g, got_x, got_g, first_t, mixed_t, second, wide, tall, back,
    w_row_t, w_depth2, w_column2, sums, land_1, land_2, land_3, land_4, sum_1, sum_2, sum_3,
    load_sem, self_sem, send_sem, recv_sem, part_send, part_recv,
):
    starts = [sum(PARTS[:part]) for part in range(len(PARTS))]
    width = 2 * seqs
    ring = ZL * CORES
    chan, me = lax.axis_index("chan"), lax.axis_index("seq")
    x, z_hi = chan // ZH, chan % ZH
    y, inner = me // ring, me % ring
    z_lo, core = inner // CORES, inner % CORES
    z = z_hi * ZL + z_lo
    local_rows = (outer + MIDDLE) // (X * CORES)

    loads = [
        pltpu.make_async_copy(source, target, load_sem.at[place])
        for place, (source, target) in enumerate((
            (signal_hbm, signal), (cotangent_hbm, cotangent),
            (depth_hbm, depth_ref), (column_hbm, column_ref), (row_hbm, row_ref),
            (depth_mask_hbm, depth_mask), (column_mask_hbm, column_mask), (row_mask_hbm, row_mask),
        ))
    ]
    for load in loads:
        load.start()

    def y_peer(step):
        return chan, lax.rem(y + step, Y) * ring + inner

    def z_peer(step):
        there = lax.rem(z + step, ZH * ZL)
        return x * ZH + there // ZL, y * ring + lax.rem(there, ZL) * CORES + core

    def x_peer(step):
        there = lax.rem(x * CORES + core + step, X * CORES)
        return there // CORES * ZH + z_hi, y * ring + z_lo * CORES + lax.rem(there, CORES)

    barrier = pltpu.get_barrier_semaphore()

    @pl.loop(0, seqs - 1)
    def _(turn):
        step = 1 + lax.rem(turn + seqs // 2 - ring // 2, seqs - 1)
        pl.semaphore_signal(barrier, inc=1, device_id=(chan, lax.rem(me + step, seqs)), device_id_type=MESH)

    greeted = seqs - 1
    for away in range(ZL):
        if ZH == 2:
            pl.semaphore_signal(
                barrier, inc=1,
                device_id=(x * ZH + 1 - z_hi, y * ring + away * CORES + core), device_id_type=MESH,
            )
            greeted += 1
    for step in range(1, X):
        for other in range(CORES):
            there = lax.rem(x + step, X) * ZH + z_hi
            pl.semaphore_signal(
                barrier, inc=1, device_id=(there, y * ring + z_lo * CORES + other), device_id_type=MESH
            )
            greeted += 1

    pick = onehot((seqs, width), same, lambda c: c // 2).astype(BF16)
    even = jnp.where(iota((1, width), 1) % 2 == 0, 1.0, 0.0).astype(BF16)
    odd = jnp.where(iota((1, width), 1) % 2 == 1, 1.0, 0.0).astype(BF16)

    def flip(read, i, start, count):
        def body(block, carry):
            value = read(pl.ds(pl.multiple_of(block * 2 * INNER, 2 * INNER), 2 * INNER))
            ones, twos = value * even, value * odd
            both = [ones[:INNER], twos[:INNER], ones[INNER:], twos[INNER:]]
            turned = dot(pick, jnp.concatenate(both, axis=0), (1, 1))
            at = pl.multiple_of(block * 2 * seqs, 2 * seqs)
            flipped[pl.ds(at, seqs), :] = turned[:, :LANES]
            flipped[pl.ds(at + seqs, seqs), :] = turned[:, LANES:]
            return carry

        at = (i * MIDDLE + start) // 2
        lax.fori_loop(at, at + count // 2, body, 0, unroll=8)

    def column_rows(i, start, count, d):
        return flipped[pl.ds((i * MIDDLE + start) * seqs + d, count, stride=seqs), :]

    def send(pack, buffer, target, start, count, slot):
        rows = pl.ds(start, count)

        def body(turn, carry):
            for place, away in enumerate(Y_ORDER):
                if away >= Y:
                    continue
                step = lax.rem(turn + place + 1, ring)
                to = lax.rem(y + away, Y) * ring + lax.rem(inner + step, ring)
                buffer[to, start : start + count, :] = pack(to).astype(BF16)

                def go():
                    pltpu.make_async_remote_copy(
                        src_ref=buffer.at[to, rows], dst_ref=target.at[me, rows],
                        send_sem=send_sem.at[slot], recv_sem=recv_sem.at[slot],
                        device_id=(chan, to), device_id_type=MESH,
                    ).start()

                if away == 0:
                    pl.when(step != 0)(go)
                else:
                    go()
            return carry

        lax.fori_loop(0, ring, body, 0)
        own = pltpu.make_async_copy(buffer.at[me, rows], target.at[me, rows], self_sem.at[slot])
        own.start()
        return own

    owns = []
    loads[0].wait()
    for part, (i, start, count) in enumerate(HEAD):
        flip(lambda rows: signal[rows, :], i, start, count)
        if part == 0:
            pl.semaphore_wait(barrier, greeted)
        owns.append(send(
            lambda d: column_rows(i, start, count, d), send_x, got_x, i * MIDDLE + start, count, part
        ))

    loads[1].wait()
    for i in range(2):
        flip(
            lambda rows: (cotangent[rows, :].astype(F32) * signal[rows, :].astype(F32)).astype(BF16),
            i, 0, MIDDLE,
        )
    for part, (start, count) in enumerate(zip(starts, PARTS)):
        def pack_part(d):
            return jnp.concatenate([column_rows(i, start, count, d) for i in range(2)], axis=0)

        owns.append(send(pack_part, send_g, got_g, 2 * start, 2 * count, len(HEAD) + part))

    for load in loads[2:]:
        load.wait()
    keep_row = spread_mask(row_mask[...], outer)
    keep_column = spread_mask(column_mask[...], MIDDLE)
    keep_depth = spread_mask(depth_mask[...], INNER)
    w_row = (row_ref[...].astype(F32) * keep_row).astype(BF16)
    w_row_t[...] = dot(onehot((outer, outer), same, same).astype(BF16), w_row, (1, 1)).astype(BF16)
    w_depth2[...] = twice((depth_ref[...].astype(F32) * keep_depth).astype(BF16))
    w_column2[...] = twice((column_ref[...].astype(F32) * keep_column).astype(BF16))

    def arrived(buffer, start, count, slot):
        owns[slot].wait()
        others = buffer.at[pl.ds(0, seqs - 1), pl.ds(start, count)]
        pltpu.make_async_copy(others, others, recv_sem.at[slot]).wait()

    for part, (i, start, count) in enumerate(HEAD):
        arrived(got_x, i * MIDDLE + start, count, part)

    def signal_side(s, carry):
        field = got_x[s]
        first = dot(field, w_depth2[...], (1, 1)).astype(BF16)
        first_t[pl.ds(pl.multiple_of(s * LANES, LANES), LANES), :] = dot(w_depth2[...], field, (1, 1)).astype(BF16)
        both = dot(w_column2[...], jnp.concatenate([field, first], axis=1), (1, 0))
        rows = pl.ds(pl.multiple_of(s * 2 * MIDDLE, 2 * MIDDLE), 2 * MIDDLE)
        tall[rows, :] = both[:, :LANES]
        wide[rows, :] = both[:, LANES:]
        return carry

    lax.fori_loop(0, seqs, signal_side, 0, unroll=4)

    same_lane = onehot((LANES, LANES), same, same).astype(BF16)

    def by_column(two, carry):
        at = [pl.ds(2 * two + j, outer, stride=MIDDLE) for j in range(2)]
        second[two] = jnp.concatenate([wide[rows, :] for rows in at], axis=1).astype(BF16)
        mixed = jnp.concatenate([tall[rows, :] for rows in at], axis=0).astype(BF16)
        mixed_t[two] = dot(same_lane, mixed, (1, 1)).astype(BF16)
        return carry

    lax.fori_loop(0, MIDDLE // 2, by_column, 0, unroll=4)

    grad_row = jnp.zeros((outer, outer), F32)
    grad_depth_t = jnp.zeros((LANES, LANES), F32)
    for part, (start, count) in enumerate(zip(starts, PARTS)):
        pair = 2 * count
        arrived(got_g, 2 * start, pair, len(HEAD) + part)

        def widen(s, carry):
            wide[pl.ds(pl.multiple_of(s * pair, pair), pair), :] = got_g[s, 2 * start : 2 * start + pair, :].astype(F32)
            return carry

        lax.fori_loop(0, seqs, widen, 0, unroll=16 if seqs % 16 == 0 else 1)

        def column_side(two, carry):
            row, depth_t = carry
            at = [pl.ds(2 * two + j, outer, stride=count) for j in range(2)]
            gated = jnp.concatenate([wide[rows, :] for rows in at], axis=1).astype(BF16)
            value = dot(w_row_t[...], gated, (1, 0))
            for j in range(2):
                back[at[j], :] = value[:, j * LANES : (j + 1) * LANES]
            value = value.astype(BF16)
            value = jnp.concatenate([value[:, :LANES], value[:, LANES:]], axis=0)
            row = row + dot(gated, second[start // 2 + two], (1, 1))
            depth_t = depth_t + dot(mixed_t[start // 2 + two], value, (1, 0))
            return row, depth_t

        grad_row, grad_depth_t = lax.fori_loop(
            0, count // 2, column_side, (grad_row, grad_depth_t), unroll=2
        )

        def back_side(two, column):
            rows = [pl.ds(pl.multiple_of((2 * two + s) * pair, pair), pair) for s in range(2)]
            value = jnp.concatenate([back[at, :] for at in rows], axis=1).astype(BF16)
            return column + dot(value, first_t[pl.ds(pl.multiple_of(two * 2 * LANES, 2 * LANES), 2 * LANES), :], (1, 0))

        column = lax.fori_loop(
            0, seqs // 2, back_side, jnp.zeros((pair, LANES), F32), unroll=min(16, seqs // 4)
        )
        sums[outer + start : outer + start + count, :MIDDLE] = column[:count, :MIDDLE] + column[count:, MIDDLE:]
    sums[:outer, :outer] = grad_row
    sums[outer:, MIDDLE:] = grad_depth_t[:INNER, :INNER] + grad_depth_t[INNER:, INNER:]

    def exchange(phase, count, peer, source, target):
        for step in FAR_FIRST:
            if step < count:
                to = peer(step)
                pltpu.make_async_remote_copy(
                    src_ref=source(to), dst_ref=target,
                    send_sem=part_send.at[phase], recv_sem=part_recv.at[phase],
                    device_id=to, device_id_type=MESH,
                ).start()

    def landed(phase, land, count):
        others = land.at[pl.ds(0, count - 1)]
        pltpu.make_async_copy(others, others, part_recv.at[phase]).wait()

    def added(land):
        total = land[0]
        for slot in range(1, land.shape[0]):
            total = total + land[slot]
        return total

    def rows_of(place):
        return pl.ds(pl.multiple_of(place * local_rows, 8), local_rows)

    def place_of(to):
        return to[0] // ZH * CORES + to[1] % CORES

    place = x * CORES + core
    exchange(0, X * CORES, x_peer, lambda to: sums.at[rows_of(place_of(to))], land_1.at[place])
    land_1[place] = sums[rows_of(place), :]
    landed(0, land_1, X * CORES)
    sum_1[...] = added(land_1)
    exchange(1, ZH * ZL, z_peer, lambda to: sum_1, land_2.at[z])
    land_2[z] = sum_1[...]
    landed(1, land_2, ZH * ZL)
    sum_2[...] = added(land_2)
    exchange(2, Y, y_peer, lambda to: sum_2, land_3.at[y])
    land_3[y] = sum_2[...]
    landed(2, land_3, Y)
    sum_3[...] = added(land_3)
    exchange(3, X * CORES, x_peer, lambda to: sum_3, land_4.at[place])
    land_4[place] = sum_3[...]
    landed(3, land_4, X * CORES)

    whole = land_4[...].reshape(outer + MIDDLE, LANES)
    inner_count = 1.0 / math.sqrt(SEQLEN * CHANNELS // MIDDLE)
    outer_count = 1.0 / math.sqrt(SEQLEN * CHANNELS // outer)
    out_row[...] = jnp.where(keep_row > 0.5, whole[:outer, :outer] * outer_count, 0.0)
    out_column[...] = jnp.where(keep_column > 0.5, whole[outer:, :MIDDLE] * inner_count, 0.0)
    out_depth[...] = jnp.where(keep_depth > 0.5, whole[outer:, MIDDLE:].T * inner_count, 0.0)

    def sent(buffer, start, count, slot):
        others = buffer.at[pl.ds(0, seqs - 1), pl.ds(start, count)]
        pltpu.make_async_copy(others, others, send_sem.at[slot]).wait()

    for part, (i, start, count) in enumerate(HEAD):
        sent(send_x, i * MIDDLE + start, count, part)
    for part, (start, count) in enumerate(zip(starts, PARTS)):
        sent(send_g, 2 * start, 2 * count, len(HEAD) + part)
    for phase, (land, count) in enumerate(
        ((land_1, X * CORES), (land_2, ZH * ZL), (land_3, Y), (land_4, X * CORES))
    ):
        others = land.at[pl.ds(0, count - 1)]
        pltpu.make_async_copy(others, others, part_send.at[phase]).wait()


def hand_over(*refs):
    sources, targets, held, sem = refs[:3], refs[3:6], refs[6:9], refs[9]
    loads = [
        pltpu.make_async_copy(source, place, sem.at[i])
        for i, (source, place) in enumerate(zip(sources, held))
    ]
    stores = [
        pltpu.make_async_copy(place, target, sem.at[3 + i])
        for i, (place, target) in enumerate(zip(held, targets))
    ]
    for load in loads:
        load.start()
    for load, store in zip(loads, stores):
        load.wait()
        store.start()
    for store in stores:
        store.wait()


def per_device(
    signal, cotangent, depth_factor, column_factor, row_factor, depth_mask, column_mask, row_mask
):
    seqs = Y * ZL * CORES
    outer = row_factor.shape[0]
    rows, width = signal.shape
    local_rows = (outer + MIDDLE) // (X * CORES)
    vmem = pl.BlockSpec(memory_space=pltpu.VMEM)
    hbm = pl.BlockSpec(memory_space=pltpu.HBM)
    shapes = (
        jax.ShapeDtypeStruct((INNER, INNER), F32),
        jax.ShapeDtypeStruct((MIDDLE, MIDDLE), F32),
        jax.ShapeDtypeStruct((outer, outer), F32),
    )
    results = pl.pallas_call(
        functools.partial(kernel, seqs, outer),
        out_shape=shapes,
        in_specs=[hbm] * 8,
        out_specs=(vmem, vmem, vmem),
        scratch_shapes=[
            pltpu.VMEM((rows, width), BF16),
            pltpu.VMEM((rows, width), BF16),
        ] + [
            pltpu.VMEM(a.shape, a.dtype)
            for a in (depth_factor, column_factor, row_factor, depth_mask, column_mask, row_mask)
        ] + [
            pltpu.VMEM((2 * MIDDLE * seqs + seqs, LANES), F32),
            pltpu.VMEM((seqs, 2 * MIDDLE, LANES), BF16),
            pltpu.VMEM((seqs, 2 * MIDDLE, LANES), BF16),
            pltpu.VMEM((seqs, 2 * MIDDLE, LANES), BF16),
            pltpu.VMEM((seqs, 2 * MIDDLE, LANES), BF16),
            pltpu.VMEM((seqs * LANES, 2 * MIDDLE), BF16),
            pltpu.VMEM((MIDDLE // 2, LANES, 2 * outer), BF16),
            pltpu.VMEM((MIDDLE // 2, outer, 2 * LANES), BF16),
            pltpu.VMEM((outer * MIDDLE + MIDDLE, LANES), F32),
            pltpu.VMEM((outer * MIDDLE + MIDDLE, LANES), F32),
            pltpu.VMEM((outer * max(PARTS) + max(PARTS), LANES), F32),
            pltpu.VMEM((outer, outer), BF16),
            pltpu.VMEM((LANES, LANES), BF16),
            pltpu.VMEM((LANES, LANES), BF16),
            pltpu.VMEM((outer + MIDDLE, LANES), F32),
            pltpu.VMEM((X * CORES, local_rows, LANES), F32),
            pltpu.VMEM((ZH * ZL, local_rows, LANES), F32),
            pltpu.VMEM((Y, local_rows, LANES), F32),
            pltpu.VMEM((X * CORES, local_rows, LANES), F32),
            pltpu.VMEM((local_rows, LANES), F32),
            pltpu.VMEM((local_rows, LANES), F32),
            pltpu.VMEM((local_rows, LANES), F32),
            pltpu.SemaphoreType.DMA((8,)),
            pltpu.SemaphoreType.DMA((len(HEAD) + len(PARTS),)),
            pltpu.SemaphoreType.DMA((len(HEAD) + len(PARTS),)),
            pltpu.SemaphoreType.DMA((len(HEAD) + len(PARTS),)),
            pltpu.SemaphoreType.DMA((4,)),
            pltpu.SemaphoreType.DMA((4,)),
        ],
        compiler_params=pltpu.CompilerParams(
            collective_id=0, has_side_effects=True, vmem_limit_bytes=60 * 2**20
        ),
        cost_estimate=pl.CostEstimate(flops=1_300_000_000, bytes_accessed=4 * 2**20, transcendentals=0),
    )(signal, cotangent, depth_factor, column_factor, row_factor, depth_mask, column_mask, row_mask)
    return pl.pallas_call(
        hand_over,
        out_shape=shapes,
        in_specs=[hbm] * 3,
        out_specs=(hbm, hbm, hbm),
        scratch_shapes=[pltpu.VMEM(a.shape, a.dtype) for a in shapes] + [pltpu.SemaphoreType.DMA((6,))],
        compiler_params=pltpu.CompilerParams(vmem_limit_bytes=60 * 2**20),
    )(*results)


def solution(mesh):
    in_specs = (P("seq", "chan"), P("seq", "chan"), P(), P(), P(), P(), P(), P())
    out_specs = (P(), P(), P())
    return jax.shard_map(
        per_device, mesh=mesh, in_specs=in_specs, out_specs=out_specs, check_vma=False
    )
```

```python
import functools
import math

import jax
import jax.numpy as jnp
from jax import lax
from jax.experimental import pallas as pl
from jax.experimental.pallas import tpu as pltpu
from jax.sharding import PartitionSpec as P

CHANNELS = 1024
SEQLEN = 524288
MIDDLE = 64
INNER = 64
LANES = 128
X, ZH, Y, ZL, CORES = 4, 2, 8, 4, 2
PARTS = (16, 16, 16, 8, 8)
HEAD = ((0, 0, 16), (0, 16, 48), (1, 0, 64))
Y_ORDER = (1, 7, 2, 6, 3, 5, 4, 0)
FAR_FIRST = (4, 3, 5, 2, 6, 1, 7)
F32, BF16 = jnp.float32, jnp.bfloat16
MESH = pl.DeviceIdType.MESH


def dot(a, b, contract):
    return lax.dot_general(a, b, ((contract[:1], contract[1:]), ((), ())), preferred_element_type=F32)


def iota(shape, axis):
    return lax.broadcasted_iota(jnp.int32, shape, axis)


def onehot(shape, left, right):
    return jnp.where(left(iota(shape, 0)) == right(iota(shape, 1)), 1.0, 0.0)


def same(value):
    return value


def spread_mask(mask, size):
    tiles = mask.shape[0]
    side = size // tiles
    ones = jnp.where(mask == 1, 1.0, 0.0)
    rows = onehot((size, tiles), lambda r: r // side, same)
    columns = onehot((tiles, size), same, lambda c: c // side)
    return dot(dot(rows, ones, (1, 0)), columns, (1, 0))


def twice(weight):
    size = weight.shape[0]
    rows = onehot((2 * size, size), lambda r: r % size, same).astype(BF16)
    columns = onehot((size, 2 * size), same, lambda c: c % size).astype(BF16)
    full = dot(dot(rows, weight, (1, 0)).astype(BF16), columns, (1, 0))
    return (full * onehot(full.shape, lambda r: r // size, lambda c: c // size)).astype(BF16)


def kernel(
    seqs, outer,
    signal_hbm, cotangent_hbm, depth_hbm, column_hbm, row_hbm, depth_mask_hbm, column_mask_hbm, row_mask_hbm,
    out_depth, out_column, out_row,
    signal, cotangent, depth_ref, column_ref, row_ref, depth_mask, column_mask, row_mask,
    flipped, send_x, send_g, got_x, got_g, first_t, mixed_t, second, wide, tall, back,
    w_row_t, w_depth2, w_column2, sums, land_1, land_2, land_3, land_4, sum_1, sum_2, sum_3,
    load_sem, self_sem, send_sem, recv_sem, part_send, part_recv,
):
    starts = [sum(PARTS[:part]) for part in range(len(PARTS))]
    width = 2 * seqs
    ring = ZL * CORES
    chan, me = lax.axis_index("chan"), lax.axis_index("seq")
    x, z_hi = chan // ZH, chan % ZH
    y, inner = me // ring, me % ring
    z_lo, core = inner // CORES, inner % CORES
    z = z_hi * ZL + z_lo
    local_rows = (outer + MIDDLE) // (X * CORES)

    loads = [
        pltpu.make_async_copy(source, target, load_sem.at[place])
        for place, (source, target) in enumerate((
            (signal_hbm, signal), (cotangent_hbm, cotangent),
            (depth_hbm, depth_ref), (column_hbm, column_ref), (row_hbm, row_ref),
            (depth_mask_hbm, depth_mask), (column_mask_hbm, column_mask), (row_mask_hbm, row_mask),
        ))
    ]
    loads[0].start()

    def y_peer(step):
        return chan, lax.rem(y + step, Y) * ring + inner

    def z_peer(step):
        there = lax.rem(z + step, ZH * ZL)
        return x * ZH + there // ZL, y * ring + lax.rem(there, ZL) * CORES + core

    def x_peer(step):
        there = lax.rem(x * CORES + core + step, X * CORES)
        return there // CORES * ZH + z_hi, y * ring + z_lo * CORES + lax.rem(there, CORES)

    barrier = pltpu.get_barrier_semaphore()

    @pl.loop(0, seqs - 1)
    def _(turn):
        step = 1 + lax.rem(turn + seqs // 2 - ring // 2, seqs - 1)
        pl.semaphore_signal(barrier, inc=1, device_id=(chan, lax.rem(me + step, seqs)), device_id_type=MESH)

    greeted = seqs - 1
    for away in range(ZL):
        if ZH == 2:
            pl.semaphore_signal(
                barrier, inc=1,
                device_id=(x * ZH + 1 - z_hi, y * ring + away * CORES + core), device_id_type=MESH,
            )
            greeted += 1
    for step in range(1, X):
        for other in range(CORES):
            there = lax.rem(x + step, X) * ZH + z_hi
            pl.semaphore_signal(
                barrier, inc=1, device_id=(there, y * ring + z_lo * CORES + other), device_id_type=MESH
            )
            greeted += 1

    for load in loads[1:]:
        load.start()

    pick = onehot((seqs, width), same, lambda c: c // 2).astype(BF16)
    even = jnp.where(iota((1, width), 1) % 2 == 0, 1.0, 0.0).astype(BF16)
    odd = jnp.where(iota((1, width), 1) % 2 == 1, 1.0, 0.0).astype(BF16)

    def flip(read, i, start, count):
        def body(block, carry):
            value = read(pl.ds(pl.multiple_of(block * 2 * INNER, 2 * INNER), 2 * INNER))
            ones, twos = value * even, value * odd
            both = [ones[:INNER], twos[:INNER], ones[INNER:], twos[INNER:]]
            turned = dot(pick, jnp.concatenate(both, axis=0), (1, 1))
            at = pl.multiple_of(block * 2 * seqs, 2 * seqs)
            flipped[pl.ds(at, seqs), :] = turned[:, :LANES]
            flipped[pl.ds(at + seqs, seqs), :] = turned[:, LANES:]
            return carry

        at = (i * MIDDLE + start) // 2
        lax.fori_loop(at, at + count // 2, body, 0, unroll=8)

    def column_rows(i, start, count, d):
        return flipped[pl.ds((i * MIDDLE + start) * seqs + d, count, stride=seqs), :]

    def send(pack, buffer, target, start, count, slot):
        rows = pl.ds(start, count)

        def body(turn, carry):
            for place, away in enumerate(Y_ORDER):
                if away >= Y:
                    continue
                step = lax.rem(turn + place + 1, ring)
                to = lax.rem(y + away, Y) * ring + lax.rem(inner + step, ring)
                buffer[to, start : start + count, :] = pack(to).astype(BF16)

                def go():
                    pltpu.make_async_remote_copy(
                        src_ref=buffer.at[to, rows], dst_ref=target.at[me, rows],
                        send_sem=send_sem.at[slot], recv_sem=recv_sem.at[slot],
                        device_id=(chan, to), device_id_type=MESH,
                    ).start()

                if away == 0:
                    pl.when(step != 0)(go)
                else:
                    go()
            return carry

        lax.fori_loop(0, ring, body, 0)
        own = pltpu.make_async_copy(buffer.at[me, rows], target.at[me, rows], self_sem.at[slot])
        own.start()
        return own

    owns = []
    loads[0].wait()
    for part, (i, start, count) in enumerate(HEAD):
        flip(lambda rows: signal[rows, :], i, start, count)
        if part == 0:
            pl.semaphore_wait(barrier, greeted)
        owns.append(send(
            lambda d: column_rows(i, start, count, d), send_x, got_x, i * MIDDLE + start, count, part
        ))

    loads[1].wait()
    for i in range(2):
        flip(
            lambda rows: (cotangent[rows, :].astype(F32) * signal[rows, :].astype(F32)).astype(BF16),
            i, 0, MIDDLE,
        )
    for part, (start, count) in enumerate(zip(starts, PARTS)):
        def pack_part(d):
            return jnp.concatenate([column_rows(i, start, count, d) for i in range(2)], axis=0)

        owns.append(send(pack_part, send_g, got_g, 2 * start, 2 * count, len(HEAD) + part))

    for load in loads[2:]:
        load.wait()
    keep_row = spread_mask(row_mask[...], outer)
    keep_column = spread_mask(column_mask[...], MIDDLE)
    keep_depth = spread_mask(depth_mask[...], INNER)
    w_row = (row_ref[...].astype(F32) * keep_row).astype(BF16)
    w_row_t[...] = dot(onehot((outer, outer), same, same).astype(BF16), w_row, (1, 1)).astype(BF16)
    w_depth2[...] = twice((depth_ref[...].astype(F32) * keep_depth).astype(BF16))
    w_column2[...] = twice((column_ref[...].astype(F32) * keep_column).astype(BF16))

    def arrived(buffer, start, count, slot):
        owns[slot].wait()
        others = buffer.at[pl.ds(0, seqs - 1), pl.ds(start, count)]
        pltpu.make_async_copy(others, others, recv_sem.at[slot]).wait()

    for part, (i, start, count) in enumerate(HEAD):
        arrived(got_x, i * MIDDLE + start, count, part)

    def signal_side(s, carry):
        field = got_x[s]
        first = dot(field, w_depth2[...], (1, 1)).astype(BF16)
        first_t[pl.ds(pl.multiple_of(s * LANES, LANES), LANES), :] = dot(w_depth2[...], field, (1, 1)).astype(BF16)
        both = dot(w_column2[...], jnp.concatenate([field, first], axis=1), (1, 0))
        rows = pl.ds(pl.multiple_of(s * 2 * MIDDLE, 2 * MIDDLE), 2 * MIDDLE)
        tall[rows, :] = both[:, :LANES]
        wide[rows, :] = both[:, LANES:]
        return carry

    lax.fori_loop(0, seqs, signal_side, 0, unroll=4)

    same_lane = onehot((LANES, LANES), same, same).astype(BF16)

    def by_column(two, carry):
        at = [pl.ds(2 * two + j, outer, stride=MIDDLE) for j in range(2)]
        second[two] = jnp.concatenate([wide[rows, :] for rows in at], axis=1).astype(BF16)
        mixed = jnp.concatenate([tall[rows, :] for rows in at], axis=0).astype(BF16)
        mixed_t[two] = dot(same_lane, mixed, (1, 1)).astype(BF16)
        return carry

    lax.fori_loop(0, MIDDLE // 2, by_column, 0, unroll=4)

    grad_row = jnp.zeros((outer, outer), F32)
    grad_depth_t = jnp.zeros((LANES, LANES), F32)
    for part, (start, count) in enumerate(zip(starts, PARTS)):
        pair = 2 * count
        arrived(got_g, 2 * start, pair, len(HEAD) + part)

        def widen(s, carry):
            wide[pl.ds(pl.multiple_of(s * pair, pair), pair), :] = got_g[s, 2 * start : 2 * start + pair, :].astype(F32)
            return carry

        lax.fori_loop(0, seqs, widen, 0, unroll=16 if seqs % 16 == 0 else 1)

        def column_side(two, carry):
            row, depth_t = carry
            at = [pl.ds(2 * two + j, outer, stride=count) for j in range(2)]
            gated = jnp.concatenate([wide[rows, :] for rows in at], axis=1).astype(BF16)
            value = dot(w_row_t[...], gated, (1, 0))
            for j in range(2):
                back[at[j], :] = value[:, j * LANES : (j + 1) * LANES]
            value = value.astype(BF16)
            value = jnp.concatenate([value[:, :LANES], value[:, LANES:]], axis=0)
            row = row + dot(gated, second[start // 2 + two], (1, 1))
            depth_t = depth_t + dot(mixed_t[start // 2 + two], value, (1, 0))
            return row, depth_t

        grad_row, grad_depth_t = lax.fori_loop(
            0, count // 2, column_side, (grad_row, grad_depth_t), unroll=2
        )

        def back_side(two, column):
            rows = [pl.ds(pl.multiple_of((2 * two + s) * pair, pair), pair) for s in range(2)]
            value = jnp.concatenate([back[at, :] for at in rows], axis=1).astype(BF16)
            return column + dot(value, first_t[pl.ds(pl.multiple_of(two * 2 * LANES, 2 * LANES), 2 * LANES), :], (1, 0))

        column = lax.fori_loop(
            0, seqs // 2, back_side, jnp.zeros((pair, LANES), F32), unroll=min(16, seqs // 4)
        )
        sums[outer + start : outer + start + count, :MIDDLE] = column[:count, :MIDDLE] + column[count:, MIDDLE:]
    sums[:outer, :outer] = grad_row
    sums[outer:, MIDDLE:] = grad_depth_t[:INNER, :INNER] + grad_depth_t[INNER:, INNER:]

    def exchange(phase, count, peer, source, target):
        for step in FAR_FIRST:
            if step < count:
                to = peer(step)
                pltpu.make_async_remote_copy(
                    src_ref=source(to), dst_ref=target,
                    send_sem=part_send.at[phase], recv_sem=part_recv.at[phase],
                    device_id=to, device_id_type=MESH,
                ).start()

    def landed(phase, land, count):
        others = land.at[pl.ds(0, count - 1)]
        pltpu.make_async_copy(others, others, part_recv.at[phase]).wait()

    def added(land):
        total = land[0]
        for slot in range(1, land.shape[0]):
            total = total + land[slot]
        return total

    def rows_of(place):
        return pl.ds(pl.multiple_of(place * local_rows, 8), local_rows)

    def place_of(to):
        return to[0] // ZH * CORES + to[1] % CORES

    place = x * CORES + core
    exchange(0, X * CORES, x_peer, lambda to: sums.at[rows_of(place_of(to))], land_1.at[place])
    land_1[place] = sums[rows_of(place), :]
    landed(0, land_1, X * CORES)
    sum_1[...] = added(land_1)
    exchange(1, ZH * ZL, z_peer, lambda to: sum_1, land_2.at[z])
    land_2[z] = sum_1[...]
    landed(1, land_2, ZH * ZL)
    sum_2[...] = added(land_2)
    exchange(2, Y, y_peer, lambda to: sum_2, land_3.at[y])
    land_3[y] = sum_2[...]
    landed(2, land_3, Y)
    sum_3[...] = added(land_3)
    exchange(3, X * CORES, x_peer, lambda to: sum_3, land_4.at[place])
    land_4[place] = sum_3[...]
    landed(3, land_4, X * CORES)

    whole = land_4[...].reshape(outer + MIDDLE, LANES)
    inner_count = 1.0 / math.sqrt(SEQLEN * CHANNELS // MIDDLE)
    outer_count = 1.0 / math.sqrt(SEQLEN * CHANNELS // outer)
    out_row[...] = jnp.where(keep_row > 0.5, whole[:outer, :outer] * outer_count, 0.0)
    out_column[...] = jnp.where(keep_column > 0.5, whole[outer:, :MIDDLE] * inner_count, 0.0)
    out_depth[...] = jnp.where(keep_depth > 0.5, whole[outer:, MIDDLE:].T * inner_count, 0.0)

    def sent(buffer, start, count, slot):
        others = buffer.at[pl.ds(0, seqs - 1), pl.ds(start, count)]
        pltpu.make_async_copy(others, others, send_sem.at[slot]).wait()

    for part, (i, start, count) in enumerate(HEAD):
        sent(send_x, i * MIDDLE + start, count, part)
    for part, (start, count) in enumerate(zip(starts, PARTS)):
        sent(send_g, 2 * start, 2 * count, len(HEAD) + part)
    for phase, (land, count) in enumerate(
        ((land_1, X * CORES), (land_2, ZH * ZL), (land_3, Y), (land_4, X * CORES))
    ):
        others = land.at[pl.ds(0, count - 1)]
        pltpu.make_async_copy(others, others, part_send.at[phase]).wait()


def hand_over(*refs):
    sources, targets, held, sem = refs[:3], refs[3:6], refs[6:9], refs[9]
    loads = [
        pltpu.make_async_copy(source, place, sem.at[i])
        for i, (source, place) in enumerate(zip(sources, held))
    ]
    stores = [
        pltpu.make_async_copy(place, target, sem.at[3 + i])
        for i, (place, target) in enumerate(zip(held, targets))
    ]
    for load in loads:
        load.start()
    for load, store in zip(loads, stores):
        load.wait()
        store.start()
    for store in stores:
        store.wait()


def per_device(
    signal, cotangent, depth_factor, column_factor, row_factor, depth_mask, column_mask, row_mask
):
    seqs = Y * ZL * CORES
    outer = row_factor.shape[0]
    rows, width = signal.shape
    local_rows = (outer + MIDDLE) // (X * CORES)
    vmem = pl.BlockSpec(memory_space=pltpu.VMEM)
    hbm = pl.BlockSpec(memory_space=pltpu.HBM)
    shapes = (
        jax.ShapeDtypeStruct((INNER, INNER), F32),
        jax.ShapeDtypeStruct((MIDDLE, MIDDLE), F32),
        jax.ShapeDtypeStruct((outer, outer), F32),
    )
    results = pl.pallas_call(
        functools.partial(kernel, seqs, outer),
        out_shape=shapes,
        in_specs=[hbm] * 8,
        out_specs=(vmem, vmem, vmem),
        scratch_shapes=[
            pltpu.VMEM((rows, width), BF16),
            pltpu.VMEM((rows, width), BF16),
        ] + [
            pltpu.VMEM(a.shape, a.dtype)
            for a in (depth_factor, column_factor, row_factor, depth_mask, column_mask, row_mask)
        ] + [
            pltpu.VMEM((2 * MIDDLE * seqs + seqs, LANES), F32),
            pltpu.VMEM((seqs, 2 * MIDDLE, LANES), BF16),
            pltpu.VMEM((seqs, 2 * MIDDLE, LANES), BF16),
            pltpu.VMEM((seqs, 2 * MIDDLE, LANES), BF16),
            pltpu.VMEM((seqs, 2 * MIDDLE, LANES), BF16),
            pltpu.VMEM((seqs * LANES, 2 * MIDDLE), BF16),
            pltpu.VMEM((MIDDLE // 2, LANES, 2 * outer), BF16),
            pltpu.VMEM((MIDDLE // 2, outer, 2 * LANES), BF16),
            pltpu.VMEM((outer * MIDDLE + MIDDLE, LANES), F32),
            pltpu.VMEM((outer * MIDDLE + MIDDLE, LANES), F32),
            pltpu.VMEM((outer * max(PARTS) + max(PARTS), LANES), F32),
            pltpu.VMEM((outer, outer), BF16),
            pltpu.VMEM((LANES, LANES), BF16),
            pltpu.VMEM((LANES, LANES), BF16),
            pltpu.VMEM((outer + MIDDLE, LANES), F32),
            pltpu.VMEM((X * CORES, local_rows, LANES), F32),
            pltpu.VMEM((ZH * ZL, local_rows, LANES), F32),
            pltpu.VMEM((Y, local_rows, LANES), F32),
            pltpu.VMEM((X * CORES, local_rows, LANES), F32),
            pltpu.VMEM((local_rows, LANES), F32),
            pltpu.VMEM((local_rows, LANES), F32),
            pltpu.VMEM((local_rows, LANES), F32),
            pltpu.SemaphoreType.DMA((8,)),
            pltpu.SemaphoreType.DMA((len(HEAD) + len(PARTS),)),
            pltpu.SemaphoreType.DMA((len(HEAD) + len(PARTS),)),
            pltpu.SemaphoreType.DMA((len(HEAD) + len(PARTS),)),
            pltpu.SemaphoreType.DMA((4,)),
            pltpu.SemaphoreType.DMA((4,)),
        ],
        compiler_params=pltpu.CompilerParams(
            collective_id=0, has_side_effects=True, vmem_limit_bytes=60 * 2**20
        ),
        cost_estimate=pl.CostEstimate(flops=1_300_000_000, bytes_accessed=4 * 2**20, transcendentals=0),
    )(signal, cotangent, depth_factor, column_factor, row_factor, depth_mask, column_mask, row_mask)
    return pl.pallas_call(
        hand_over,
        out_shape=shapes,
        in_specs=[hbm] * 3,
        out_specs=(hbm, hbm, hbm),
        scratch_shapes=[pltpu.VMEM(a.shape, a.dtype) for a in shapes] + [pltpu.SemaphoreType.DMA((6,))],
        compiler_params=pltpu.CompilerParams(vmem_limit_bytes=60 * 2**20),
    )(*results)


def solution(mesh):
    in_specs = (P("seq", "chan"), P("seq", "chan"), P(), P(), P(), P(), P(), P())
    out_specs = (P(), P(), P())
    return jax.shard_map(
        per_device, mesh=mesh, in_specs=in_specs, out_specs=out_specs, check_vma=False
    )
```
